128 devices in a mesh: seq: 32 (over z, y_lo, x), tp: 4 (over y_hi, core).
Axes of the slice: x: 4, y: 4 (y_hi: 2, y_lo: 2; y = y_hi * 2 + y_lo), z: 4, core: 2. Of those that a mesh axis runs over, the one named last changes fastest.
Arguments:
- tokens: bfloat16 [16384, 4096], P(('seq', 'tp')), may hold values from -64 to 64, as said below
- joined_projection_weight: bfloat16 [4096, 6144], P(None, 'tp'), may hold values from -0.09375 to 0.09375
- adapter_down_weight: bfloat16 [4096, 64], replicated, may hold values from -0.09375 to 0.09375
- adapter_up_weight: bfloat16 [64, 6144], P(None, 'tp'), may hold values from -0.75 to 0.75
- document_index: int32 [16384], replicated, may hold values from 0 to 3, as said below
- query_to_key_head: int32 [32], replicated, may hold values from 0 to 7, as said below
Outputs:
- context: bfloat16 [16384, 4096], P(('seq', 'tp'))
The draws below stay inside these ranges and needn't reach their ends.
Inputs may be any that keep to these rules, and one draw needn't show every extreme that they name: `tokens`: rows of order one, except in the hidden draw where some rows have larger scales. `query_to_key_head`: each of 0 to 7 is named by exactly 4 query heads. `document_index`: never falling, starting at 0; each of the 4 documents covers 16384 / 16 or more positions.
All inputs are finite; a program needn't handle non-finite values.
Results may differ from the reference program's by a relative error of at most 0.012.
The reference program's roundings to bfloat16 on the way count: a program that leaves them out, or rounds other values in their place, can miss the bound.
Values may be sent and summed in bfloat16 or wider, within the bound.
No kernel may reach another device: no remote copies, remote signals or barrier semaphores. Data moves between devices by JAX's collectives and lax.ppermute only.
A program may use at most 128 MiB of HBM per device.

```python
import jax
import jax.numpy as jnp
from jax import lax

MODEL_WIDTH = 4096
H = 32
KV = 8
DH = 128
ADAPTER_RANK = 64
DOCS = 4
S = 16384
JOINED_COLUMNS = 6144
N_TP = 4


def draw_tokens(key, part):
    noise_key = jax.random.fold_in(key, 0)
    drawn = jax.random.normal(noise_key, (S, MODEL_WIDTH), jnp.float32)
    return jnp.clip(drawn, -64.0, 64.0).astype(jnp.bfloat16)


def draw_document_index(key, part):
    length_key = jax.random.fold_in(key, 7)
    lengths = jax.random.randint(length_key, (DOCS - 1,), S // 16, 5 * S // 16, dtype=jnp.int32)
    bounds = jnp.cumsum(lengths).astype(jnp.int32)
    places = jnp.arange(S, dtype=jnp.int32)
    return jnp.sum((places[:, None] >= bounds[None, :]).astype(jnp.int32), axis=1).astype(jnp.int32)


def draw_query_to_key_head(key, part):
    order = jax.random.permutation(key, H)
    return (order % KV).astype(jnp.int32)


def level_of(rng, extent, shards, least, largest):
    level, own = 1.0, jax.random.fold_in(rng, 6)
    for dim, blocks in shards:
        heights = jnp.exp(jax.random.uniform(jax.random.fold_in(own, dim), (blocks,), jnp.float32, least / len(shards), largest / len(shards)))
        level = level * jnp.repeat(heights, extent[dim] // blocks).reshape([-1 if axis == dim else 1 for axis in range(len(extent))])
    return level


def gaussian(key, dims, spread, limit, shards=(), kind=jnp.bfloat16):
    gain = level_of(key, dims, shards, -0.22, 0.18) if shards else 1.0
    result = jax.random.normal(key, dims, jnp.float32) * spread * gain
    return jnp.minimum(jnp.maximum(result, -limit), limit).astype(kind)


def setup_inputs(seed: int = 0) -> dict:
    splits = jax.random.split(jax.random.key(seed), 7)
    return {
        "tokens": draw_tokens(jax.random.fold_in(splits[6], 71), 0),
        "joined_projection_weight": gaussian(splits[1], (MODEL_WIDTH, JOINED_COLUMNS), MODEL_WIDTH ** -0.5, 0.09375, ((1, 4),)),
        "adapter_down_weight": gaussian(splits[2], (MODEL_WIDTH, ADAPTER_RANK), MODEL_WIDTH ** -0.5, 0.09375),
        "adapter_up_weight": gaussian(splits[3], (ADAPTER_RANK, JOINED_COLUMNS), ADAPTER_RANK ** -0.5, 0.75, ((1, 4),)),
        "document_index": draw_document_index(jax.random.fold_in(splits[6], 71), 0),
        "query_to_key_head": draw_query_to_key_head(jax.random.fold_in(splits[6], 71), 0),
    }


ADAPTER_SCALE = 0.5
THETA = 500000.0


def rotate(values, places):
    half_dim = values.shape[-1] // 2
    frequency = THETA ** (-(jnp.arange(half_dim, dtype=jnp.float32) * 2.0) / values.shape[-1])
    angles = places[:, None] * frequency[None, :]
    cosine = jnp.cos(angles)[:, None, :]
    sine_part = jnp.sin(angles)[:, None, :]
    front_half = values[..., :half_dim]
    back_half = values[..., half_dim:]
    return jnp.concatenate([front_half * cosine - back_half * sine_part, back_half * cosine + front_half * sine_part], axis=-1)


def reference(tokens, joined_projection_weight, adapter_down_weight, adapter_up_weight, document_index, query_to_key_head):
    projected_rows = jnp.dot(tokens, joined_projection_weight, preferred_element_type=jnp.float32)
    adapter_middle = jnp.dot(tokens, adapter_down_weight, preferred_element_type=jnp.float32).astype(jnp.bfloat16)
    joined_output = projected_rows + ADAPTER_SCALE * jnp.dot(adapter_middle, adapter_up_weight, preferred_element_type=jnp.float32)
    query_group = H // N_TP
    key_group = KV // N_TP
    grouped = joined_output.reshape(S, N_TP, (query_group + 2 * key_group) * DH)
    queries = grouped[:, :, :query_group * DH].reshape(S, H, DH)
    keys = grouped[:, :, query_group * DH:(query_group + key_group) * DH].reshape(S, KV, DH)
    values = grouped[:, :, (query_group + key_group) * DH:].reshape(S, KV, DH)
    places = jnp.arange(S, dtype=jnp.int32).astype(jnp.float32)
    q_rot = rotate(queries, places).astype(jnp.bfloat16)
    k_rot = rotate(keys, places).astype(jnp.bfloat16)
    v_half = values.astype(jnp.bfloat16)
    k_head = k_rot[:, query_to_key_head]
    v_head = v_half[:, query_to_key_head]
    scale = DH ** -0.5
    query_block = min(1024, S)
    key_places = jnp.arange(S, dtype=jnp.int32)

    def head_out(head_index):
        q_one = lax.dynamic_index_in_dim(q_rot, head_index, 1, keepdims=False)
        k_one = lax.dynamic_index_in_dim(k_head, head_index, 1, keepdims=False)
        v_one = lax.dynamic_index_in_dim(v_head, head_index, 1, keepdims=False)

        def block_out(block_index):
            start = (block_index * query_block).astype(jnp.int32)
            q_tile = lax.dynamic_slice_in_dim(q_one, start, query_block, 0)
            tile_places = start + jnp.arange(query_block, dtype=jnp.int32)
            tile_segments = lax.dynamic_slice_in_dim(document_index, start, query_block, 0)
            scores = jnp.dot(q_tile, k_one.T, preferred_element_type=jnp.float32) * scale
            allowed = (key_places[None, :] <= tile_places[:, None]) & (document_index[None, :] == tile_segments[:, None])
            scores = jnp.where(allowed, scores, -jnp.inf)
            row_max = jnp.max(scores, axis=-1, keepdims=True)
            powers = jnp.exp(scores - row_max)
            weights = powers.astype(jnp.bfloat16)
            numer = jnp.dot(weights, v_one, preferred_element_type=jnp.float32)
            return (numer / jnp.sum(powers, axis=-1, keepdims=True)).astype(jnp.bfloat16)

        return lax.map(block_out, jnp.arange(S // query_block, dtype=jnp.int32)).reshape(S, DH)

    per_head = lax.map(head_out, jnp.arange(H, dtype=jnp.int32))
    return jnp.transpose(per_head, (1, 0, 2)).reshape(S, H * DH)
```

```python
import functools

import jax
import jax.numpy as jnp
from jax import lax
from jax.experimental import pallas as pl
from jax.experimental.pallas import tpu as pltpu
from jax.sharding import Mesh
from jax.sharding import PartitionSpec as P

H = 32
KV = 8
DH = 128
BLK = 128
THETA = 500000.0
ADAPTER_SCALE = 0.5
NEG_BIG = -1e30
DOCS = 4

NZ, NYL, NX, NYH, NC = 4, 2, 4, 2, 2
ALL = ("z", "yl", "x", "yh", "c")
BF = jnp.bfloat16
F32 = jnp.float32
KEYS = 512


def flat(z, yl, x, yh, c):
    return (((z * NYL + yl) * NX + x) * NYH + yh) * NC + c


def every():
    for z in range(NZ):
        for yl in range(NYL):
            for x in range(NX):
                for yh in range(NYH):
                    for c in range(NC):
                        yield z, yl, x, yh, c


CROSS = [(flat(*d), flat(d[0], 1 - d[1], d[2], 1 - d[3], d[4])) for d in every()]
CROSS_OTHER = [(flat(*d), flat(d[0], 1 - d[1], d[2], 1 - d[3], 1 - d[4])) for d in every()]
SWAP = [(0, 1), (1, 0)]
GROUPS = [
    [flat(z, yl0 ^ yh, (x0 + z) % NX, yh, c) for z in range(NZ) for yh in range(NYH)]
    for x0 in range(NX)
    for yl0 in range(NYL)
    for c in range(NC)
]


def rope_tables(blocks):
    half = DH // 2
    frequency = THETA ** (-(jnp.arange(half, dtype=F32) * 2.0) / DH)
    places = (blocks[:, None] * BLK + jnp.arange(BLK, dtype=jnp.int32)[None, :]).reshape(-1).astype(F32)
    angles = places[:, None] * frequency[None, :]
    cosine, sine = jnp.cos(angles), jnp.sin(angles)
    return jnp.concatenate([cosine, cosine], axis=1), jnp.concatenate([-sine, sine], axis=1)


def rotated(part, cosine, sine):
    return part * cosine + pltpu.roll(part, DH // 2, 1) * sine


def kv_kernel(x0, x1, w, down, up, cosine, sine, out, mid_out, rows, mid):
    step = pl.program_id(0)

    @pl.when(step == 0)
    def _():
        rows[:BLK] = x0[...]
        rows[BLK:] = x1[...]
        mid[...] = jnp.dot(rows[...], down[...], preferred_element_type=F32).astype(BF)
        mid_out[...] = mid[...]

    acc = jnp.dot(rows[...], w[...], preferred_element_type=F32)
    acc = acc + ADAPTER_SCALE * jnp.dot(mid[...], up[...], preferred_element_type=F32)

    @pl.when(step == 0)
    def _():
        for head in range(2):
            part = rotated(acc[:, head * DH:(head + 1) * DH], cosine[...], sine[...]).astype(BF)
            for block in range(2):
                out[block, head, 0] = part[block * BLK:(block + 1) * BLK]

    @pl.when(step == 1)
    def _():
        for head in range(2):
            part = acc[:, head * DH:(head + 1) * DH].astype(BF)
            for block in range(2):
                out[block, head, 0] = part[block * BLK:(block + 1) * BLK]


def q_kernel(x0, x1, mid, w, up, cosine, sine, out, rows):
    step = pl.program_id(0)

    @pl.when(step == 0)
    def _():
        rows[:BLK] = x0[...]
        rows[BLK:] = x1[...]

    acc = jnp.dot(rows[...], w[...], preferred_element_type=F32)
    acc = acc + ADAPTER_SCALE * jnp.dot(mid[...], up[...], preferred_element_type=F32)
    for head in range(2):
        part = rotated(acc[:, head * DH:(head + 1) * DH], cosine[...], sine[...]).astype(BF)
        for block in range(2):
            out[block, head] = part[block * BLK:(block + 1) * BLK]


def whole(shape):
    return pl.BlockSpec(shape, lambda *_: (0,) * len(shape))


def project_kv(x0, x1, w, down, up, cosine, sine):
    width = x0.shape[1]
    rank = down.shape[1]
    return pl.pallas_call(
        kv_kernel,
        grid=(2,),
        in_specs=[
            whole((BLK, width)),
            whole((BLK, width)),
            pl.BlockSpec((width, 2 * DH), lambda j: (0, 4 + j)),
            whole((width, rank)),
            pl.BlockSpec((rank, 2 * DH), lambda j: (0, 4 + j)),
            whole((2 * BLK, DH)),
            whole((2 * BLK, DH)),
        ],
        out_specs=[
            pl.BlockSpec((2, 2, 1, BLK, DH), lambda j: (0, 0, j, 0, 0)),
            whole((2 * BLK, rank)),
        ],
        out_shape=[
            jax.ShapeDtypeStruct((2, 2, 2, BLK, DH), BF),
            jax.ShapeDtypeStruct((2 * BLK, rank), BF),
        ],
        scratch_shapes=[pltpu.VMEM((2 * BLK, width), BF), pltpu.VMEM((2 * BLK, rank), BF)],
        compiler_params=pltpu.CompilerParams(vmem_limit_bytes=40 * 2**20),
        cost_estimate=pl.CostEstimate(
            flops=2 * 2 * BLK * width * 4 * DH, bytes_accessed=width * 4 * DH * 2, transcendentals=0
        ),
        name="project_kv",
    )(x0, x1, w, down, up, cosine, sine)


def project_q(x0, x1, mid, w, up, cosine, sine):
    width = x0.shape[1]
    rank = mid.shape[1]
    return pl.pallas_call(
        q_kernel,
        grid=(4,),
        in_specs=[
            whole((BLK, width)),
            whole((BLK, width)),
            whole((2 * BLK, rank)),
            pl.BlockSpec((width, 2 * DH), lambda j: (0, j)),
            pl.BlockSpec((rank, 2 * DH), lambda j: (0, j)),
            whole((2 * BLK, DH)),
            whole((2 * BLK, DH)),
        ],
        out_specs=pl.BlockSpec((2, 2, BLK, DH), lambda j: (0, j, 0, 0)),
        out_shape=jax.ShapeDtypeStruct((2, 8, BLK, DH), BF),
        scratch_shapes=[pltpu.VMEM((2 * BLK, width), BF)],
        compiler_params=pltpu.CompilerParams(vmem_limit_bytes=40 * 2**20),
        cost_estimate=pl.CostEstimate(
            flops=2 * 2 * BLK * width * 8 * DH, bytes_accessed=width * 8 * DH * 2, transcendentals=0
        ),
        name="project_q",
    )(x0, x1, mid, w, up, cosine, sine)


def sort_kernel(source, a, b, c, d, out):
    for slot in range(H):
        pick = source[slot]
        which = pick // 8
        inner = pick % 8
        for k, ref in enumerate((a, b, c, d)):

            @pl.when(which == k)
            def _(ref=ref):
                out[slot // 4, slot % 4] = ref[inner]


def sort_heads(source, parts):
    return pl.pallas_call(
        sort_kernel,
        in_specs=[pl.BlockSpec(memory_space=pltpu.SMEM)] + [pl.BlockSpec(memory_space=pltpu.VMEM)] * 4,
        out_specs=pl.BlockSpec(memory_space=pltpu.VMEM),
        out_shape=jax.ShapeDtypeStruct((KV, 4, BLK, DH), BF),
        compiler_params=pltpu.CompilerParams(vmem_limit_bytes=16 * 2**20),
        cost_estimate=pl.CostEstimate(flops=0, bytes_accessed=2 * H * BLK * DH * 2, transcendentals=0),
        name="sort_heads",
    )(source, *parts)


def unsort_kernel(slots, a, out):
    for head in range(H):
        slot = slots[head]
        out[:, head * DH:(head + 1) * DH] = a[slot // 4, slot % 4]


def unsort_heads(slots, a):
    return pl.pallas_call(
        unsort_kernel,
        in_specs=[pl.BlockSpec(memory_space=pltpu.SMEM), pl.BlockSpec(memory_space=pltpu.VMEM)],
        out_specs=pl.BlockSpec(memory_space=pltpu.VMEM),
        out_shape=jax.ShapeDtypeStruct((BLK, H * DH), BF),
        compiler_params=pltpu.CompilerParams(vmem_limit_bytes=16 * 2**20),
        cost_estimate=pl.CostEstimate(flops=0, bytes_accessed=2 * H * BLK * DH * 2, transcendentals=0),
        name="unsort_heads",
    )(slots, a)


def attend_kernel(blocks, starts, own_half, q_ref, kv0, kv1, out, keys, values, sems, top, total, acc):
    tile = pl.program_id(0)
    yh = own_half[0]

    @pl.when(tile == 0)
    def _():
        copies = []
        for z in range(NZ):
            for yl in range(NYL):
                for kind, dst in enumerate((keys, values)):
                    for stage, src in enumerate((kv0, kv1)):
                        at_half = yh if stage == 0 else 1 - yh
                        at_low = yl if stage == 0 else 1 - yl
                        copies.append(
                            pltpu.make_async_copy(
                                src.at[:, yl, :, z, kind],
                                dst.at[pl.ds((z * NYL + at_low) * NX, NX), at_half],
                                sems.at[len(copies)],
                            )
                        )
        for copy in copies:
            copy.start()
        for copy in copies:
            copy.wait()

    rows = 4 * BLK
    block = blocks[tile]
    first = block * BLK
    last = first + BLK - 1

    def start_of(place):
        found = jnp.int32(0)
        for d in range(1, DOCS):
            found = jnp.maximum(found, jnp.where(starts[d] <= place, starts[d], 0))
        return found

    low = start_of(first) // KEYS
    high_start = start_of(last)
    diagonal = first // KEYS
    factor = (DH ** -0.5) * 1.4426950408889634

    top[...] = jnp.full(top.shape, NEG_BIG, F32)
    total[...] = jnp.zeros(total.shape, F32)
    acc[...] = jnp.zeros(acc.shape, F32)
    q = q_ref[0].reshape(rows, DH)

    def step(index, masked):
        k_tile = keys[index].reshape(KEYS, DH)
        v_tile = values[index].reshape(KEYS, DH)
        scores = lax.dot_general(q, k_tile, (((1,), (1,)), ((), ())), preferred_element_type=F32) * factor
        if masked:
            place = first + lax.broadcasted_iota(jnp.int32, (rows, 1), 0) % BLK
            begin = jnp.zeros((rows, 1), jnp.int32)
            for d in range(1, DOCS):
                begin = jnp.maximum(begin, jnp.where(place >= starts[d], starts[d], 0))
            at = index * KEYS + lax.broadcasted_iota(jnp.int32, (rows, KEYS), 1)
            scores = jnp.where((at <= place) & (at >= begin), scores, -jnp.inf)
        old = top[...]
        new = jnp.maximum(old, jnp.max(scores, axis=1, keepdims=True))
        shrink = jnp.exp2(old - new)
        powers = jnp.exp2(scores - new[:, :1])
        top[...] = new
        total[...] = total[...] * shrink + jnp.sum(powers, axis=1, keepdims=True)
        acc[...] = acc[...] * shrink + jnp.dot(powers.astype(BF), v_tile, preferred_element_type=F32)

    def body(index, carry):
        masked = (index == diagonal) | (index * KEYS < high_start)

        @pl.when(masked)
        def _():
            step(index, True)

        @pl.when(jnp.logical_not(masked))
        def _():
            step(index, False)

        return carry

    lax.fori_loop(low, diagonal + 1, body, 0)
    out[0] = (acc[...] / total[...]).astype(BF).reshape(4, BLK, DH)


def attend(blocks, starts, own_half, q, kv0, kv1):
    rows = 4 * BLK
    shape = (NX, NYL, NC, NZ, 2, BLK, DH)
    n_blocks = NZ * NYL * NX
    return pl.pallas_call(
        attend_kernel,
        grid=(8,),
        in_specs=[pl.BlockSpec(memory_space=pltpu.SMEM)] * 3
        + [
            pl.BlockSpec((1, 4, BLK, DH), lambda i: (i, 0, 0, 0)),
            pl.BlockSpec(memory_space=pl.ANY),
            pl.BlockSpec(memory_space=pl.ANY),
        ],
        out_specs=pl.BlockSpec((1, 4, BLK, DH), lambda i: (i, 0, 0, 0)),
        out_shape=jax.ShapeDtypeStruct((8, 4, BLK, DH), BF),
        scratch_shapes=[
            pltpu.VMEM((n_blocks, NYH, NC, BLK, DH), BF),
            pltpu.VMEM((n_blocks, NYH, NC, BLK, DH), BF),
            pltpu.SemaphoreType.DMA((32,)),
            pltpu.VMEM((rows, DH), F32),
            pltpu.VMEM((rows, DH), F32),
            pltpu.VMEM((rows, DH), F32),
        ],
        compiler_params=pltpu.CompilerParams(vmem_limit_bytes=40 * 2**20),
        cost_estimate=pl.CostEstimate(flops=10**10, bytes_accessed=10 * 2**20, transcendentals=10**7),
        name="attend",
    )(blocks, starts, own_half, q, kv0.reshape(shape), kv1.reshape(shape))


def per_device(tokens, w, down, up, document_index, query_to_key_head):
    z, yl, x, yh, c = (lax.axis_index(a) for a in ALL)
    block = flat(z, yl, x, yh, c)
    far_block = flat(z, 1 - yl, x, 1 - yh, c)
    other = 1 - 2 * c

    far = lax.ppermute(tokens, ALL, CROSS)
    near_pair = lax.ppermute(tokens, "c", SWAP)

    near_cos, near_sin = rope_tables(jnp.stack([block, block + other]))
    far_cos, far_sin = rope_tables(jnp.stack([far_block, far_block + other]))

    def spread_kv(kv):
        mine, theirs = kv[0], lax.ppermute(kv[1], "c", SWAP)
        heads = jnp.where(c == 0, jnp.concatenate([mine, theirs], 0), jnp.concatenate([theirs, mine], 0))
        heads = lax.all_to_all(heads, "z", split_axis=0, concat_axis=0, tiled=True)
        return lax.all_gather(heads[None], ("x", "yl", "c"), axis=0, tiled=True)

    kv_near, mid_near = project_kv(tokens, near_pair, w, down, up, near_cos, near_sin)
    kv0 = spread_kv(kv_near)
    q_near = project_q(tokens, near_pair, mid_near, w, up, near_cos, near_sin)

    far_pair = lax.ppermute(far, "c", SWAP)
    kv_far, mid_far = project_kv(far, far_pair, w, down, up, far_cos, far_sin)
    kv1 = spread_kv(kv_far)
    q_far = project_q(far, far_pair, mid_far, w, up, far_cos, far_sin)

    parts = (
        q_near[0],
        lax.ppermute(q_near[1], "c", SWAP),
        lax.ppermute(q_far[0], ALL, CROSS),
        lax.ppermute(q_far[1], ALL, CROSS_OTHER),
    )
    member = (query_to_key_head % 4) * 2 + query_to_key_head // 4
    heads = jnp.arange(H, dtype=jnp.int32)
    same = (member[None, :] == member[:, None]) & (heads[None, :] < heads[:, None])
    slots = member * 4 + jnp.sum(same.astype(jnp.int32), axis=1)
    source_of_head = ((heads // 8) ^ (yh * 2 + c)) * 8 + heads % 8
    source = jnp.sum(jnp.where(slots[None, :] == heads[:, None], source_of_head[None, :], 0), axis=1)
    sorted_q = sort_heads(source, parts)
    q = lax.all_to_all(sorted_q, ALL, split_axis=0, concat_axis=0, tiled=True, axis_index_groups=GROUPS)

    member_z = jnp.arange(8, dtype=jnp.int32) // 2
    member_yh = jnp.arange(8, dtype=jnp.int32) % 2
    blocks = flat(member_z, (yl ^ yh) ^ member_yh, (x - z + member_z) % NX, member_yh, c).astype(jnp.int32)
    starts = jnp.sum(
        (document_index[None, :] < jnp.arange(DOCS, dtype=jnp.int32)[:, None]).astype(jnp.int32), axis=1
    )
    context = attend(blocks, starts, yh[None].astype(jnp.int32), q, kv0, kv1)
    home = lax.all_to_all(context, ALL, split_axis=0, concat_axis=0, tiled=True, axis_index_groups=GROUPS)
    return unsort_heads(slots, home)


def solution(mesh):
    fine = Mesh(mesh.devices.reshape(NZ, NYL, NX, NYH, NC), ALL)
    return jax.shard_map(
        per_device,
        mesh=fine,
        in_specs=(P(ALL, None), P(None, ("yh", "c")), P(), P(None, ("yh", "c")), P(), P()),
        out_specs=P(ALL, None),
        check_vma=False,
    )
```

```python
import functools

import jax
import jax.numpy as jnp
from jax import lax
from jax.experimental import pallas as pl
from jax.experimental.pallas import tpu as pltpu
from jax.sharding import Mesh
from jax.sharding import PartitionSpec as P

H = 32
KV = 8
DH = 128
BLK = 128
THETA = 500000.0
ADAPTER_SCALE = 0.5
NEG_BIG = -1e30
DOCS = 4

NZ, NYL, NX, NYH, NC = 4, 2, 4, 2, 2
ALL = ("z", "yl", "x", "yh", "c")
BF = jnp.bfloat16
F32 = jnp.float32
WIDE = 8


def flat(z, yl, x, yh, c):
    return (((z * NYL + yl) * NX + x) * NYH + yh) * NC + c


def every():
    for z in range(NZ):
        for yl in range(NYL):
            for x in range(NX):
                for yh in range(NYH):
                    for c in range(NC):
                        yield z, yl, x, yh, c


CROSS = [(flat(*d), flat(d[0], 1 - d[1], d[2], 1 - d[3], d[4])) for d in every()]
CROSS_OTHER = [(flat(*d), flat(d[0], 1 - d[1], d[2], 1 - d[3], 1 - d[4])) for d in every()]
SWAP = [(0, 1), (1, 0)]
GROUPS = [
    [flat(z, yl0 ^ yh, (x0 + z) % NX, yh, c) for z in range(NZ) for yh in range(NYH)]
    for x0 in range(NX)
    for yl0 in range(NYL)
    for c in range(NC)
]


def rope_tables(blocks):
    half = DH // 2
    frequency = THETA ** (-(jnp.arange(half, dtype=F32) * 2.0) / DH)
    places = (blocks[:, None] * BLK + jnp.arange(BLK, dtype=jnp.int32)[None, :]).reshape(-1).astype(F32)
    angles = places[:, None] * frequency[None, :]
    cosine, sine = jnp.cos(angles), jnp.sin(angles)
    return jnp.concatenate([cosine, cosine], axis=1), jnp.concatenate([-sine, sine], axis=1)


def rotated(part, cosine, sine):
    return part * cosine + pltpu.roll(part, DH // 2, 1) * sine


def kv_kernel(x0, x1, w, down, up, cosine, sine, out, mid_out, rows, mid):
    step = pl.program_id(0)

    @pl.when(step == 0)
    def _():
        rows[:BLK] = x0[...]
        rows[BLK:] = x1[...]
        mid[...] = jnp.dot(rows[...], down[...], preferred_element_type=F32).astype(BF)
        mid_out[...] = mid[...]

    acc = jnp.dot(rows[...], w[...], preferred_element_type=F32)
    acc = acc + ADAPTER_SCALE * jnp.dot(mid[...], up[...], preferred_element_type=F32)

    @pl.when(step == 0)
    def _():
        for head in range(2):
            part = rotated(acc[:, head * DH:(head + 1) * DH], cosine[...], sine[...]).astype(BF)
            for block in range(2):
                out[block, head, 0] = part[block * BLK:(block + 1) * BLK]

    @pl.when(step == 1)
    def _():
        for head in range(2):
            part = acc[:, head * DH:(head + 1) * DH].astype(BF)
            for block in range(2):
                out[block, head, 0] = part[block * BLK:(block + 1) * BLK]


def q_kernel(x0, x1, mid, w, up, cosine, sine, out, rows):
    step = pl.program_id(0)

    @pl.when(step == 0)
    def _():
        rows[:BLK] = x0[...]
        rows[BLK:] = x1[...]

    acc = jnp.dot(rows[...], w[...], preferred_element_type=F32)
    acc = acc + ADAPTER_SCALE * jnp.dot(mid[...], up[...], preferred_element_type=F32)
    for head in range(2):
        part = rotated(acc[:, head * DH:(head + 1) * DH], cosine[...], sine[...]).astype(BF)
        for block in range(2):
            out[block, head] = part[block * BLK:(block + 1) * BLK]


def whole(shape):
    return pl.BlockSpec(shape, lambda *_: (0,) * len(shape))


def project_kv(x0, x1, w, down, up, cosine, sine):
    width = x0.shape[1]
    rank = down.shape[1]
    return pl.pallas_call(
        kv_kernel,
        grid=(2,),
        in_specs=[
            whole((BLK, width)),
            whole((BLK, width)),
            pl.BlockSpec((width, 2 * DH), lambda j: (0, 4 + j)),
            whole((width, rank)),
            pl.BlockSpec((rank, 2 * DH), lambda j: (0, 4 + j)),
            whole((2 * BLK, DH)),
            whole((2 * BLK, DH)),
        ],
        out_specs=[
            pl.BlockSpec((2, 2, 1, BLK, DH), lambda j: (0, 0, j, 0, 0)),
            whole((2 * BLK, rank)),
        ],
        out_shape=[
            jax.ShapeDtypeStruct((2, 2, 2, BLK, DH), BF),
            jax.ShapeDtypeStruct((2 * BLK, rank), BF),
        ],
        scratch_shapes=[pltpu.VMEM((2 * BLK, width), BF), pltpu.VMEM((2 * BLK, rank), BF)],
        compiler_params=pltpu.CompilerParams(vmem_limit_bytes=40 * 2**20),
        cost_estimate=pl.CostEstimate(
            flops=2 * 2 * BLK * width * 4 * DH, bytes_accessed=width * 4 * DH * 2, transcendentals=0
        ),
        name="project_kv",
    )(x0, x1, w, down, up, cosine, sine)


def project_q(x0, x1, mid, w, up, cosine, sine):
    width = x0.shape[1]
    rank = mid.shape[1]
    return pl.pallas_call(
        q_kernel,
        grid=(4,),
        in_specs=[
            whole((BLK, width)),
            whole((BLK, width)),
            whole((2 * BLK, rank)),
            pl.BlockSpec((width, 2 * DH), lambda j: (0, j)),
            pl.BlockSpec((rank, 2 * DH), lambda j: (0, j)),
            whole((2 * BLK, DH)),
            whole((2 * BLK, DH)),
        ],
        out_specs=pl.BlockSpec((2, 2, BLK, DH), lambda j: (0, j, 0, 0)),
        out_shape=jax.ShapeDtypeStruct((2, 8, BLK, DH), BF),
        scratch_shapes=[pltpu.VMEM((2 * BLK, width), BF)],
        compiler_params=pltpu.CompilerParams(vmem_limit_bytes=40 * 2**20),
        cost_estimate=pl.CostEstimate(
            flops=2 * 2 * BLK * width * 8 * DH, bytes_accessed=width * 8 * DH * 2, transcendentals=0
        ),
        name="project_q",
    )(x0, x1, mid, w, up, cosine, sine)


def sort_kernel(source, a, b, c, d, out):
    for slot in range(H):
        pick = source[slot]
        which = pick // 8
        inner = pick % 8
        for k, ref in enumerate((a, b, c, d)):

            @pl.when(which == k)
            def _(ref=ref):
                out[slot // 4, slot % 4] = ref[inner]


def sort_heads(source, parts):
    return pl.pallas_call(
        sort_kernel,
        in_specs=[pl.BlockSpec(memory_space=pltpu.SMEM)] + [pl.BlockSpec(memory_space=pltpu.VMEM)] * 4,
        out_specs=pl.BlockSpec(memory_space=pltpu.VMEM),
        out_shape=jax.ShapeDtypeStruct((KV, 4, BLK, DH), BF),
        compiler_params=pltpu.CompilerParams(vmem_limit_bytes=16 * 2**20),
        cost_estimate=pl.CostEstimate(flops=0, bytes_accessed=2 * H * BLK * DH * 2, transcendentals=0),
        name="sort_heads",
    )(source, *parts)


def unsort_kernel(slots, a, out):
    for head in range(H):
        slot = slots[head]
        out[:, head * DH:(head + 1) * DH] = a[slot // 4, slot % 4]


def unsort_heads(slots, a):
    return pl.pallas_call(
        unsort_kernel,
        in_specs=[pl.BlockSpec(memory_space=pltpu.SMEM), pl.BlockSpec(memory_space=pltpu.VMEM)],
        out_specs=pl.BlockSpec(memory_space=pltpu.VMEM),
        out_shape=jax.ShapeDtypeStruct((BLK, H * DH), BF),
        compiler_params=pltpu.CompilerParams(vmem_limit_bytes=16 * 2**20),
        cost_estimate=pl.CostEstimate(flops=0, bytes_accessed=2 * H * BLK * DH * 2, transcendentals=0),
        name="unsort_heads",
    )(slots, a)


def attend_kernel(blocks, starts, own, q_ref, kv0, kv1, out, pairs, sems, top, total, acc, floor):
    yh = own[0]

    def copies_of(z):
        return [
            pltpu.make_async_copy(src.at[:, pl.ds((own[1] - z + NZ) % NZ, 1)], pairs.at[stage, :, pl.ds(z, 1)], sems.at[2 * z + stage])
            for stage, src in enumerate((kv0, kv1))
        ]

    for z in range(NZ):
        for copy in copies_of(z):
            copy.start()

    def gathered(begin_block, width, kind):
        parts = []
        for k in range(width):
            key_block = jnp.maximum(begin_block + k, 0)
            low = (key_block // (NC * NYH * NX)) % NYL
            stage = ((key_block // NC) % NYH) ^ yh
            source = (((key_block // (NC * NYH)) % NX) * NYL + (low ^ stage)) * NC + key_block % NC
            parts.append(pairs[stage, source, key_block // (NC * NYH * NX * NYL), kind])
        return jnp.concatenate(parts, axis=0)

    def one_tile(tile):
        rows = 4 * BLK
        block = blocks[tile]
        first = block * BLK

        def start_of(place):
            found = jnp.int32(0)
            for d in range(1, DOCS):
                found = jnp.maximum(found, jnp.where(starts[d] <= place, starts[d], 0))
            return found

        span = block + 1 - start_of(first) // BLK
        latest_start = start_of(first + BLK - 1)
        factor = (DH ** -0.5) * 1.4426950408889634

        top[...] = jnp.full(top.shape, NEG_BIG, F32)
        total[...] = jnp.zeros(total.shape, F32)
        acc[...] = jnp.zeros(acc.shape, F32)
        q = q_ref[tile].reshape(rows, DH)

        place = first + lax.broadcasted_iota(jnp.int32, (rows, DH), 0) % BLK
        begin = jnp.zeros((rows, DH), jnp.int32)
        for d in range(1, DOCS):
            begin = jnp.maximum(begin, jnp.where(place >= starts[d], starts[d], 0))
        floor[...] = begin

        def step(begin_block, width, at_end, at_start):
            k_tile = gathered(begin_block, width, 0)
            v_tile = gathered(begin_block, width, 1)
            scores = lax.dot_general(q, k_tile, (((1,), (1,)), ((), ())), preferred_element_type=F32)
            parts = [scores[:, j:j + DH] * factor for j in range(0, width * BLK, DH)]
            lane = lax.broadcasted_iota(jnp.int32, (rows, DH), 1)
            if at_start:
                lowest = floor[...] - lane
                parts = [jnp.where(lowest <= (begin_block + j) * BLK, part, -jnp.inf) for j, part in enumerate(parts)]
            if at_end:
                inside = lane <= lax.broadcasted_iota(jnp.int32, (rows, DH), 0) % BLK
                parts[-1] = jnp.where(inside, parts[-1], -jnp.inf)
            old = top[...]
            peak = functools.reduce(jnp.maximum, parts)
            new = jnp.maximum(old, jnp.max(peak, axis=1, keepdims=True))
            shrink = jnp.exp2(old - new)
            powers = [jnp.exp2(part - new) for part in parts]
            top[...] = new
            total[...] = total[...] * shrink + functools.reduce(jnp.add, powers)
            weights = jnp.concatenate([p.astype(BF) for p in powers], axis=1)
            acc[...] = acc[...] * shrink + jnp.dot(weights, v_tile, preferred_element_type=F32)

        whole_steps = (span + WIDE // 2 - 1) // WIDE

        def starting(begin_block):
            return begin_block * BLK < latest_start

        def either(begin_block, width, at_end):
            early = starting(begin_block)

            @pl.when(early)
            def _():
                step(begin_block, width, at_end, True)

            @pl.when(jnp.logical_not(early))
            def _():
                step(begin_block, width, at_end, False)

        @pl.when(whole_steps > 0)
        def _():
            either(block + 1 - WIDE, WIDE, True)

        def body(index, carry):
            either(block + 1 - WIDE * (index + 1), WIDE, False)
            return carry

        lax.fori_loop(1, whole_steps, body, 0)

        left = span - WIDE * whole_steps

        @pl.when((left > 0) & (whole_steps == 0))
        def _():
            step(block + 1 - WIDE // 2, WIDE // 2, True, True)

        @pl.when((left > 0) & (whole_steps > 0))
        def _():
            step(block + 1 - WIDE * whole_steps - WIDE // 2, WIDE // 2, False, True)

        out[tile] = (acc[...] / jnp.sum(total[...], axis=1, keepdims=True)).astype(BF).reshape(4, BLK, DH)

    def pair(z, carry):
        for copy in copies_of(z):
            copy.wait()
        one_tile(2 * z)
        one_tile(2 * z + 1)
        return carry

    lax.fori_loop(0, NZ, pair, 0)


def attend(blocks, starts, own, q, kv0, kv1):
    rows = 4 * BLK
    return pl.pallas_call(
        attend_kernel,
        in_specs=[pl.BlockSpec(memory_space=pltpu.SMEM)] * 3
        + [
            pl.BlockSpec(memory_space=pltpu.VMEM),
            pl.BlockSpec(memory_space=pl.ANY),
            pl.BlockSpec(memory_space=pl.ANY),
        ],
        out_specs=pl.BlockSpec(memory_space=pltpu.VMEM),
        out_shape=jax.ShapeDtypeStruct((8, 4, BLK, DH), BF),
        scratch_shapes=[
            pltpu.VMEM((2, NX * NYL * NC, NZ, 2, BLK, DH), BF),
            pltpu.SemaphoreType.DMA((2 * NZ,)),
            pltpu.VMEM((rows, DH), F32),
            pltpu.VMEM((rows, DH), F32),
            pltpu.VMEM((rows, DH), F32),
            pltpu.VMEM((rows, DH), jnp.int32),
        ],
        compiler_params=pltpu.CompilerParams(vmem_limit_bytes=60 * 2**20),
        cost_estimate=pl.CostEstimate(flops=10**10, bytes_accessed=10 * 2**20, transcendentals=10**7),
        name="attend",
    )(blocks, starts, own, q, kv0, kv1)


def per_device(tokens, w, down, up, document_index, query_to_key_head):
    z, yl, x, yh, c = (lax.axis_index(a) for a in ALL)
    block = flat(z, yl, x, yh, c)
    far_block = flat(z, 1 - yl, x, 1 - yh, c)
    other = 1 - 2 * c

    far = lax.ppermute(tokens, ALL, CROSS)
    near_pair = lax.ppermute(tokens, "c", SWAP)

    near_cos, near_sin = rope_tables(jnp.stack([block, block + other]))
    far_cos, far_sin = rope_tables(jnp.stack([far_block, far_block + other]))

    def split_kv(kv):
        mine, theirs = kv[0], lax.ppermute(kv[1], "c", SWAP)
        heads = jnp.where(c == 0, jnp.concatenate([mine, theirs], 0), jnp.concatenate([theirs, mine], 0))
        rows = []
        for k in range(NZ):
            head = lax.dynamic_index_in_dim(heads, (z + k) % NZ, 0, keepdims=False)
            rows.append(lax.ppermute(head, "z", [(i, (i + k) % NZ) for i in range(NZ)]) if k else head)
        return jnp.stack(rows)[None]

    def spread_kv(rows):
        return lax.all_gather(rows, ("x", "yl", "c"), axis=0, tiled=True)

    kv_near, mid_near = project_kv(tokens, near_pair, w, down, up, near_cos, near_sin)
    rows_near = split_kv(kv_near)
    kv0 = spread_kv(rows_near)
    q_near = project_q(tokens, near_pair, mid_near, w, up, near_cos, near_sin)

    far, q_near, rows_near = lax.optimization_barrier((far, q_near, rows_near))
    far_pair = lax.ppermute(far, "c", SWAP)
    kv_far, mid_far = project_kv(far, far_pair, w, down, up, far_cos, far_sin)
    kv1 = spread_kv(split_kv(kv_far))
    q_far = project_q(far, far_pair, mid_far, w, up, far_cos, far_sin)

    parts = (
        q_near[0],
        lax.ppermute(q_near[1], "c", SWAP),
        lax.ppermute(q_far[0], ALL, CROSS),
        lax.ppermute(q_far[1], ALL, CROSS_OTHER),
    )
    member = (query_to_key_head % 4) * 2 + query_to_key_head // 4
    heads = jnp.arange(H, dtype=jnp.int32)
    same = (member[None, :] == member[:, None]) & (heads[None, :] < heads[:, None])
    slots = member * 4 + jnp.sum(same.astype(jnp.int32), axis=1)
    source_of_head = ((heads // 8) ^ (yh * 2 + c)) * 8 + heads % 8
    source = jnp.sum(jnp.where(slots[None, :] == heads[:, None], source_of_head[None, :], 0), axis=1)
    sorted_q = sort_heads(source, parts)
    q = lax.all_to_all(sorted_q, ALL, split_axis=0, concat_axis=0, tiled=True, axis_index_groups=GROUPS)

    member_z = jnp.arange(8, dtype=jnp.int32) // 2
    member_yh = jnp.arange(8, dtype=jnp.int32) % 2
    blocks = flat(member_z, (yl ^ yh) ^ member_yh, (x - z + member_z) % NX, member_yh, c).astype(jnp.int32)
    starts = jnp.sum(
        (document_index[None, :] < jnp.arange(DOCS, dtype=jnp.int32)[:, None]).astype(jnp.int32), axis=1
    )
    context = attend(blocks, starts, jnp.stack([yh, z]).astype(jnp.int32), q, kv0, kv1)
    home = lax.all_to_all(context, ALL, split_axis=0, concat_axis=0, tiled=True, axis_index_groups=GROUPS)
    return unsort_heads(slots, home)


def solution(mesh):
    fine = Mesh(mesh.devices.reshape(NZ, NYL, NX, NYH, NC), ALL)
    return jax.shard_map(
        per_device,
        mesh=fine,
        in_specs=(P(ALL, None), P(None, ("yh", "c")), P(), P(None, ("yh", "c")), P(), P()),
        out_specs=P(ALL, None),
        check_vma=False,
    )
```

```python
import functools

import jax
import jax.numpy as jnp
from jax import lax
from jax.experimental import pallas as pl
from jax.experimental.pallas import tpu as pltpu
from jax.sharding import Mesh
from jax.sharding import PartitionSpec as P

H = 32
KV = 8
DH = 128
BLK = 128
THETA = 500000.0
ADAPTER_SCALE = 0.5
NEG_BIG = -1e30
DOCS = 4

NZ, NYL, NX, NYH, NC = 4, 2, 4, 2, 2
ALL = ("z", "yl", "x", "yh", "c")
BF = jnp.bfloat16
F32 = jnp.float32
WIDE = 8


def flat(z, yl, x, yh, c):
    return (((z * NYL + yl) * NX + x) * NYH + yh) * NC + c


def every():
    for z in range(NZ):
        for yl in range(NYL):
            for x in range(NX):
                for yh in range(NYH):
                    for c in range(NC):
                        yield z, yl, x, yh, c


CROSS = [(flat(*d), flat(d[0], 1 - d[1], d[2], 1 - d[3], d[4])) for d in every()]
CROSS_OTHER = [(flat(*d), flat(d[0], 1 - d[1], d[2], 1 - d[3], 1 - d[4])) for d in every()]
SWAP = [(0, 1), (1, 0)]
GROUPS = [
    [flat(z, yl0 ^ yh, (x0 + z) % NX, yh, c) for z in range(NZ) for yh in range(NYH)]
    for x0 in range(NX)
    for yl0 in range(NYL)
    for c in range(NC)
]


def rope_tables(blocks):
    half = DH // 2
    frequency = THETA ** (-(jnp.arange(half, dtype=F32) * 2.0) / DH)
    places = (blocks[:, None] * BLK + jnp.arange(BLK, dtype=jnp.int32)[None, :]).reshape(-1).astype(F32)
    angles = places[:, None] * frequency[None, :]
    cosine, sine = jnp.cos(angles), jnp.sin(angles)
    return jnp.concatenate([cosine, cosine], axis=1), jnp.concatenate([-sine, sine], axis=1)


def rotated(part, cosine, sine):
    return part * cosine + pltpu.roll(part, DH // 2, 1) * sine


def gather_rows(x0, x1, rows):
    rows[:BLK] = x0[...]
    rows[BLK:] = x1[...]


def kv_kernel(makes_mid, x0, x1, w, low, up, cosine, sine, out, *rest):
    step = pl.program_id(0)
    if makes_mid:
        mid, rows = rest
    else:
        mid, (rows,) = low, rest

    @pl.when(step == 0)
    def _():
        gather_rows(x0, x1, rows)
        if makes_mid:
            mid[...] = jnp.dot(rows[...], low[...], preferred_element_type=F32).astype(BF)

    acc = jnp.dot(rows[...], w[...], preferred_element_type=F32)
    acc = acc + ADAPTER_SCALE * jnp.dot(mid[...], up[...], preferred_element_type=F32)

    @pl.when(step == 0)
    def _():
        for head in range(2):
            part = rotated(acc[:, head * DH:(head + 1) * DH], cosine[...], sine[...]).astype(BF)
            for block in range(2):
                out[block, head, 0] = part[block * BLK:(block + 1) * BLK]

    @pl.when(step == 1)
    def _():
        for head in range(2):
            part = acc[:, head * DH:(head + 1) * DH].astype(BF)
            for block in range(2):
                out[block, head, 0] = part[block * BLK:(block + 1) * BLK]


def q_kernel(makes_mid, x0, x1, w, low, up, cosine, sine, out, *rest):
    step = pl.program_id(0)
    if makes_mid:
        mid, rows = rest
    else:
        mid, (rows,) = low, rest

    @pl.when(step == 0)
    def _():
        gather_rows(x0, x1, rows)
        if makes_mid:
            mid[...] = jnp.dot(rows[...], low[...], preferred_element_type=F32).astype(BF)

    acc = jnp.dot(rows[...], w[...], preferred_element_type=F32)
    acc = acc + ADAPTER_SCALE * jnp.dot(mid[...], up[...], preferred_element_type=F32)
    for head in range(2):
        part = rotated(acc[:, head * DH:(head + 1) * DH], cosine[...], sine[...]).astype(BF)
        for block in range(2):
            out[block, head] = part[block * BLK:(block + 1) * BLK]


def both_kernel(x0, x1, w, low, up, cosine, sine, out_q, out_kv, mid, rows):
    step = pl.program_id(0)

    @pl.when(step == 0)
    def _():
        gather_rows(x0, x1, rows)
        mid[...] = jnp.dot(rows[...], low[...], preferred_element_type=F32).astype(BF)

    acc = jnp.dot(rows[...], w[...], preferred_element_type=F32)
    acc = acc + ADAPTER_SCALE * jnp.dot(mid[...], up[...], preferred_element_type=F32)

    @pl.when(step < 4)
    def _():
        for head in range(2):
            part = rotated(acc[:, head * DH:(head + 1) * DH], cosine[...], sine[...]).astype(BF)
            for block in range(2):
                out_q[block, head] = part[block * BLK:(block + 1) * BLK]

    @pl.when(step == 4)
    def _():
        for head in range(2):
            part = rotated(acc[:, head * DH:(head + 1) * DH], cosine[...], sine[...]).astype(BF)
            for block in range(2):
                out_kv[block, head, 0] = part[block * BLK:(block + 1) * BLK]

    @pl.when(step == 5)
    def _():
        for head in range(2):
            part = acc[:, head * DH:(head + 1) * DH].astype(BF)
            for block in range(2):
                out_kv[block, head, 0] = part[block * BLK:(block + 1) * BLK]


def project_both(x0, x1, w, down, up, cosine, sine):
    width = x0.shape[1]
    rank = down.shape[1]
    return pl.pallas_call(
        both_kernel,
        grid=(6,),
        in_specs=[
            whole((BLK, width)),
            whole((BLK, width)),
            pl.BlockSpec((width, 2 * DH), lambda j: (0, j)),
            whole(down.shape),
            pl.BlockSpec((rank, 2 * DH), lambda j: (0, j)),
            whole((2 * BLK, DH)),
            whole((2 * BLK, DH)),
        ],
        out_specs=[
            pl.BlockSpec((2, 2, BLK, DH), lambda j: (0, jnp.minimum(j, 3), 0, 0)),
            pl.BlockSpec((2, 2, 1, BLK, DH), lambda j: (0, 0, jnp.maximum(j - 4, 0), 0, 0)),
        ],
        out_shape=[
            jax.ShapeDtypeStruct((2, 8, BLK, DH), BF),
            jax.ShapeDtypeStruct((2, 2, 2, BLK, DH), BF),
        ],
        scratch_shapes=[pltpu.VMEM((2 * BLK, rank), BF), pltpu.VMEM((2 * BLK, width), BF)],
        compiler_params=pltpu.CompilerParams(vmem_limit_bytes=40 * 2**20),
        cost_estimate=pl.CostEstimate(
            flops=2 * 2 * BLK * width * 12 * DH, bytes_accessed=width * 12 * DH * 2, transcendentals=0
        ),
        name="project_both",
    )(x0, x1, w, down, up, cosine, sine)


def whole(shape):
    return pl.BlockSpec(shape, lambda *_: (0,) * len(shape))


def project(for_keys, x0, x1, w, low, up, cosine, sine):
    width = x0.shape[1]
    rank = low.shape[1]
    makes_mid = low.shape[0] == width
    steps, base = (2, 4) if for_keys else (4, 0)
    if for_keys:
        out_spec = pl.BlockSpec((2, 2, 1, BLK, DH), lambda j: (0, 0, j, 0, 0))
        out_shape = jax.ShapeDtypeStruct((2, 2, 2, BLK, DH), BF)
    else:
        out_spec = pl.BlockSpec((2, 2, BLK, DH), lambda j: (0, j, 0, 0))
        out_shape = jax.ShapeDtypeStruct((2, 8, BLK, DH), BF)
    mid_spec, mid_shape = [], []
    if makes_mid:
        mid_spec, mid_shape = [whole((2 * BLK, rank))], [jax.ShapeDtypeStruct((2 * BLK, rank), BF)]
    made = pl.pallas_call(
        functools.partial(kv_kernel if for_keys else q_kernel, makes_mid),
        grid=(steps,),
        in_specs=[
            whole((BLK, width)),
            whole((BLK, width)),
            pl.BlockSpec((width, 2 * DH), lambda j: (0, base + j)),
            whole(low.shape),
            pl.BlockSpec((rank, 2 * DH), lambda j: (0, base + j)),
            whole((2 * BLK, DH)),
            whole((2 * BLK, DH)),
        ],
        out_specs=[out_spec] + mid_spec,
        out_shape=[out_shape] + mid_shape,
        scratch_shapes=[pltpu.VMEM((2 * BLK, width), BF)],
        compiler_params=pltpu.CompilerParams(vmem_limit_bytes=40 * 2**20),
        cost_estimate=pl.CostEstimate(
            flops=2 * 2 * BLK * width * 2 * DH * steps, bytes_accessed=width * 2 * DH * steps * 2, transcendentals=0
        ),
        name="project_kv" if for_keys else "project_q",
    )(x0, x1, w, low, up, cosine, sine)
    return made if makes_mid else made[0]


def sort_kernel(source, a, b, c, d, out):
    for slot in range(H):
        pick = source[slot]
        which = pick // 8
        inner = pick % 8
        for k, ref in enumerate((a, b, c, d)):

            @pl.when(which == k)
            def _(ref=ref):
                out[slot // 4, slot % 4] = ref[inner]


def sort_heads(source, parts):
    return pl.pallas_call(
        sort_kernel,
        in_specs=[pl.BlockSpec(memory_space=pltpu.SMEM)] + [pl.BlockSpec(memory_space=pltpu.VMEM)] * 4,
        out_specs=pl.BlockSpec(memory_space=pltpu.VMEM),
        out_shape=jax.ShapeDtypeStruct((KV, 4, BLK, DH), BF),
        compiler_params=pltpu.CompilerParams(vmem_limit_bytes=16 * 2**20),
        cost_estimate=pl.CostEstimate(flops=0, bytes_accessed=2 * H * BLK * DH * 2, transcendentals=0),
        name="sort_heads",
    )(source, *parts)


def unsort_kernel(slots, a, out):
    for head in range(H):
        slot = slots[head]
        out[:, head * DH:(head + 1) * DH] = a[slot // 4, slot % 4]


def unsort_heads(slots, a):
    return pl.pallas_call(
        unsort_kernel,
        in_specs=[pl.BlockSpec(memory_space=pltpu.SMEM), pl.BlockSpec(memory_space=pltpu.VMEM)],
        out_specs=pl.BlockSpec(memory_space=pltpu.VMEM),
        out_shape=jax.ShapeDtypeStruct((BLK, H * DH), BF),
        compiler_params=pltpu.CompilerParams(vmem_limit_bytes=16 * 2**20),
        cost_estimate=pl.CostEstimate(flops=0, bytes_accessed=2 * H * BLK * DH * 2, transcendentals=0),
        name="unsort_heads",
    )(slots, a)


def attend_kernel(blocks, starts, own, q_ref, kv, out, pairs, sems, top, total, acc, floor):
    yh = own[0]

    def copy_of(z):
        return pltpu.make_async_copy(
            kv.at[:, pl.ds((own[1] - z + NZ) % NZ, 1)], pairs.at[:, pl.ds(z, 1)], sems.at[z]
        )

    for z in range(NZ):
        copy_of(z).start()

    def gathered(begin_block, width, kind):
        parts = []
        for k in range(width):
            key_block = jnp.maximum(begin_block + k, 0)
            low = (key_block // (NC * NYH * NX)) % NYL
            stage = ((key_block // NC) % NYH) ^ yh
            source = (((key_block // (NC * NYH)) % NX) * NYL + (low ^ stage)) * NC + key_block % NC
            parts.append(pairs[source, key_block // (NC * NYH * NX * NYL), stage, kind])
        return jnp.concatenate(parts, axis=0)

    def one_tile(tile):
        rows = 4 * BLK
        block = blocks[tile]
        first = block * BLK

        def start_of(place):
            found = jnp.int32(0)
            for d in range(1, DOCS):
                found = jnp.maximum(found, jnp.where(starts[d] <= place, starts[d], 0))
            return found

        span = block + 1 - start_of(first) // BLK
        latest_start = start_of(first + BLK - 1)
        factor = (DH ** -0.5) * 1.4426950408889634

        top[...] = jnp.full(top.shape, NEG_BIG, F32)
        total[...] = jnp.zeros(total.shape, F32)
        acc[...] = jnp.zeros(acc.shape, F32)
        q = q_ref[tile].reshape(rows, DH)

        place = first + lax.broadcasted_iota(jnp.int32, (rows, DH), 0) % BLK
        begin = jnp.zeros((rows, DH), jnp.int32)
        for d in range(1, DOCS):
            begin = jnp.maximum(begin, jnp.where(place >= starts[d], starts[d], 0))
        floor[...] = begin

        def step(begin_block, width, at_end, at_start):
            k_tile = gathered(begin_block, width, 0)
            v_tile = gathered(begin_block, width, 1)
            scores = lax.dot_general(q, k_tile, (((1,), (1,)), ((), ())), preferred_element_type=F32)
            parts = [scores[:, j:j + DH] * factor for j in range(0, width * BLK, DH)]
            lane = lax.broadcasted_iota(jnp.int32, (rows, DH), 1)
            if at_start:
                lowest = floor[...] - lane
                parts = [jnp.where(lowest <= (begin_block + j) * BLK, part, -jnp.inf) for j, part in enumerate(parts)]
            if at_end:
                inside = lane <= lax.broadcasted_iota(jnp.int32, (rows, DH), 0) % BLK
                parts[-1] = jnp.where(inside, parts[-1], -jnp.inf)
            old = top[...]
            peak = functools.reduce(jnp.maximum, parts)
            new = jnp.maximum(old, jnp.max(peak, axis=1, keepdims=True))
            shrink = jnp.exp2(old - new)
            powers = [jnp.exp2(part - new) for part in parts]
            top[...] = new
            total[...] = total[...] * shrink + functools.reduce(jnp.add, powers)
            weights = jnp.concatenate([p.astype(BF) for p in powers], axis=1)
            acc[...] = acc[...] * shrink + jnp.dot(weights, v_tile, preferred_element_type=F32)

        whole_steps = (span + WIDE // 2 - 1) // WIDE

        def starting(begin_block):
            return begin_block * BLK < latest_start

        def either(begin_block, width, at_end):
            early = starting(begin_block)

            @pl.when(early)
            def _():
                step(begin_block, width, at_end, True)

            @pl.when(jnp.logical_not(early))
            def _():
                step(begin_block, width, at_end, False)

        @pl.when(whole_steps > 0)
        def _():
            either(block + 1 - WIDE, WIDE, True)

        def body(index, carry):
            either(block + 1 - WIDE * (index + 1), WIDE, False)
            return carry

        lax.fori_loop(1, whole_steps, body, 0)

        left = span - WIDE * whole_steps

        @pl.when((left > 0) & (whole_steps == 0))
        def _():
            step(block + 1 - WIDE // 2, WIDE // 2, True, True)

        @pl.when((left > 0) & (whole_steps > 0))
        def _():
            step(block + 1 - WIDE * whole_steps - WIDE // 2, WIDE // 2, False, True)

        out[tile] = (acc[...] / jnp.sum(total[...], axis=1, keepdims=True)).astype(BF).reshape(4, BLK, DH)

    def pair(z, carry):
        copy_of(z).wait()
        one_tile(2 * z)
        one_tile(2 * z + 1)
        return carry

    lax.fori_loop(0, NZ, pair, 0)


def attend(blocks, starts, own, q, kv):
    rows = 4 * BLK
    return pl.pallas_call(
        attend_kernel,
        in_specs=[pl.BlockSpec(memory_space=pltpu.SMEM)] * 3
        + [
            pl.BlockSpec(memory_space=pltpu.VMEM),
            pl.BlockSpec(memory_space=pl.ANY),
        ],
        out_specs=pl.BlockSpec(memory_space=pltpu.VMEM),
        out_shape=jax.ShapeDtypeStruct((8, 4, BLK, DH), BF),
        scratch_shapes=[
            pltpu.VMEM((NX * NYL * NC, NZ, 2, 2, BLK, DH), BF),
            pltpu.SemaphoreType.DMA((NZ,)),
            pltpu.VMEM((rows, DH), F32),
            pltpu.VMEM((rows, DH), F32),
            pltpu.VMEM((rows, DH), F32),
            pltpu.VMEM((rows, DH), jnp.int32),
        ],
        compiler_params=pltpu.CompilerParams(vmem_limit_bytes=60 * 2**20),
        cost_estimate=pl.CostEstimate(flops=10**10, bytes_accessed=10 * 2**20, transcendentals=10**7),
        name="attend",
    )(blocks, starts, own, q, kv)


def per_device(tokens, w, down, up, document_index, query_to_key_head):
    z, yl, x, yh, c = (lax.axis_index(a) for a in ALL)
    block = flat(z, yl, x, yh, c)
    far_block = flat(z, 1 - yl, x, 1 - yh, c)
    other = 1 - 2 * c

    far = lax.ppermute(tokens, ALL, CROSS)
    near_pair = lax.ppermute(tokens, "c", SWAP)

    near_cos, near_sin = rope_tables(jnp.stack([block, block + other]))
    far_cos, far_sin = rope_tables(jnp.stack([far_block, far_block + other]))

    def split_kv(near, far):
        mine, theirs = jnp.stack([near[0], far[0]], 1), lax.ppermute(jnp.stack([near[1], far[1]], 1), "c", SWAP)
        heads = jnp.where(c == 0, jnp.concatenate([mine, theirs], 0), jnp.concatenate([theirs, mine], 0))
        rows = []
        for k in range(NZ):
            head = lax.dynamic_index_in_dim(heads, (z + k) % NZ, 0, keepdims=False)
            rows.append(lax.ppermute(head, "z", [(i, (i + k) % NZ) for i in range(NZ)]) if k else head)
        return jnp.stack(rows)[None]

    q_near, kv_near = project_both(tokens, near_pair, w, down, up, near_cos, near_sin)
    far, q_near, kv_near = lax.optimization_barrier((far, q_near, kv_near))
    far_pair = lax.ppermute(far, "c", SWAP)
    q_far, mid_far = project(False, far, far_pair, w, down, up, far_cos, far_sin)
    home_c = lax.ppermute(q_far[0], ALL, CROSS)
    home_d = lax.ppermute(q_far[1], ALL, CROSS_OTHER)
    kv_far = project(True, far, far_pair, w, mid_far, up, far_cos, far_sin)
    kv_far, home_c = lax.optimization_barrier((kv_far, home_c))
    rows, home_d = lax.optimization_barrier((split_kv(kv_near, kv_far), home_d))
    kv = lax.all_gather(rows, ("x", "yl", "c"), axis=0, tiled=True)

    parts = (
        q_near[0],
        lax.ppermute(q_near[1], "c", SWAP),
        home_c,
        home_d,
    )
    member = (query_to_key_head % 4) * 2 + query_to_key_head // 4
    heads = jnp.arange(H, dtype=jnp.int32)
    same = (member[None, :] == member[:, None]) & (heads[None, :] < heads[:, None])
    slots = member * 4 + jnp.sum(same.astype(jnp.int32), axis=1)
    source_of_head = ((heads // 8) ^ (yh * 2 + c)) * 8 + heads % 8
    source = jnp.sum(jnp.where(slots[None, :] == heads[:, None], source_of_head[None, :], 0), axis=1)
    sorted_q = sort_heads(source, parts)
    q = lax.all_to_all(sorted_q, ALL, split_axis=0, concat_axis=0, tiled=True, axis_index_groups=GROUPS)

    member_z = jnp.arange(8, dtype=jnp.int32) // 2
    member_yh = jnp.arange(8, dtype=jnp.int32) % 2
    blocks = flat(member_z, (yl ^ yh) ^ member_yh, (x - z + member_z) % NX, member_yh, c).astype(jnp.int32)
    starts = jnp.sum(
        (document_index[None, :] < jnp.arange(DOCS, dtype=jnp.int32)[:, None]).astype(jnp.int32), axis=1
    )
    context = attend(blocks, starts, jnp.stack([yh, z]).astype(jnp.int32), q, kv)
    home = lax.all_to_all(context, ALL, split_axis=0, concat_axis=0, tiled=True, axis_index_groups=GROUPS)
    return unsort_heads(slots, home)


def solution(mesh):
    fine = Mesh(mesh.devices.reshape(NZ, NYL, NX, NYH, NC), ALL)
    return jax.shard_map(
        per_device,
        mesh=fine,
        in_specs=(P(ALL, None), P(None, ("yh", "c")), P(), P(None, ("yh", "c")), P(), P()),
        out_specs=P(ALL, None),
        check_vma=False,
    )
```

```python
import functools

import jax
import jax.numpy as jnp
from jax import lax
from jax.experimental import pallas as pl
from jax.experimental.pallas import tpu as pltpu
from jax.sharding import Mesh
from jax.sharding import PartitionSpec as P

H = 32
KV = 8
DH = 128
BLK = 128
THETA = 500000.0
ADAPTER_SCALE = 0.5
NEG_BIG = -1e30
DOCS = 4

NZ, NYL, NX, NYH, NC = 4, 2, 4, 2, 2
ALL = ("z", "yl", "x", "yh", "c")
BF = jnp.bfloat16
F32 = jnp.float32
WIDE = 8


def flat(z, yl, x, yh, c):
    return (((z * NYL + yl) * NX + x) * NYH + yh) * NC + c


def every():
    for z in range(NZ):
        for yl in range(NYL):
            for x in range(NX):
                for yh in range(NYH):
                    for c in range(NC):
                        yield z, yl, x, yh, c


CROSS = [(flat(*d), flat(d[0], 1 - d[1], d[2], 1 - d[3], d[4])) for d in every()]
CROSS_OTHER = [(flat(*d), flat(d[0], 1 - d[1], d[2], 1 - d[3], 1 - d[4])) for d in every()]
SWAP = [(0, 1), (1, 0)]
GROUPS = [
    [flat(z, yl0 ^ yh, (x0 + z) % NX, yh, c) for z in range(NZ) for yh in range(NYH)]
    for x0 in range(NX)
    for yl0 in range(NYL)
    for c in range(NC)
]


def rope_tables(blocks):
    half = DH // 2
    frequency = THETA ** (-(jnp.arange(half, dtype=F32) * 2.0) / DH)
    places = (blocks[:, None] * BLK + jnp.arange(BLK, dtype=jnp.int32)[None, :]).reshape(-1).astype(F32)
    angles = places[:, None] * frequency[None, :]
    cosine, sine = jnp.cos(angles), jnp.sin(angles)
    return jnp.concatenate([cosine, cosine], axis=1), jnp.concatenate([-sine, sine], axis=1)


def rotated(part, cosine, sine):
    return part * cosine + pltpu.roll(part, DH // 2, 1) * sine


def gather_rows(x0, x1, rows):
    rows[:BLK] = x0[...]
    rows[BLK:] = x1[...]


def kv_kernel(makes_mid, x0, x1, w, low, up, cosine, sine, out, *rest):
    step = pl.program_id(0)
    if makes_mid:
        mid, rows = rest
    else:
        mid, (rows,) = low, rest

    @pl.when(step == 0)
    def _():
        gather_rows(x0, x1, rows)
        if makes_mid:
            mid[...] = jnp.dot(rows[...], low[...], preferred_element_type=F32).astype(BF)

    acc = jnp.dot(rows[...], w[...], preferred_element_type=F32)
    acc = acc + ADAPTER_SCALE * jnp.dot(mid[...], up[...], preferred_element_type=F32)

    @pl.when(step == 0)
    def _():
        for head in range(2):
            part = rotated(acc[:, head * DH:(head + 1) * DH], cosine[...], sine[...]).astype(BF)
            for block in range(2):
                out[block, head, 0] = part[block * BLK:(block + 1) * BLK]

    @pl.when(step == 1)
    def _():
        for head in range(2):
            part = acc[:, head * DH:(head + 1) * DH].astype(BF)
            for block in range(2):
                out[block, head, 0] = part[block * BLK:(block + 1) * BLK]


def q_kernel(makes_mid, x0, x1, w, low, up, cosine, sine, out, *rest):
    step = pl.program_id(0)
    if makes_mid:
        mid, rows = rest
    else:
        mid, (rows,) = low, rest

    @pl.when(step == 0)
    def _():
        gather_rows(x0, x1, rows)
        if makes_mid:
            mid[...] = jnp.dot(rows[...], low[...], preferred_element_type=F32).astype(BF)

    acc = jnp.dot(rows[...], w[...], preferred_element_type=F32)
    acc = acc + ADAPTER_SCALE * jnp.dot(mid[...], up[...], preferred_element_type=F32)
    for head in range(2):
        part = rotated(acc[:, head * DH:(head + 1) * DH], cosine[...], sine[...]).astype(BF)
        for block in range(2):
            out[block, head] = part[block * BLK:(block + 1) * BLK]


def both_kernel(x0, x1, w, low, up, cosine, sine, out_q, out_kv, mid, rows):
    step = pl.program_id(0)

    @pl.when(step == 0)
    def _():
        gather_rows(x0, x1, rows)
        mid[...] = jnp.dot(rows[...], low[...], preferred_element_type=F32).astype(BF)

    acc = jnp.dot(rows[...], w[...], preferred_element_type=F32)
    acc = acc + ADAPTER_SCALE * jnp.dot(mid[...], up[...], preferred_element_type=F32)

    @pl.when(step < 4)
    def _():
        for head in range(2):
            part = rotated(acc[:, head * DH:(head + 1) * DH], cosine[...], sine[...]).astype(BF)
            for block in range(2):
                out_q[block, head] = part[block * BLK:(block + 1) * BLK]

    @pl.when(step == 4)
    def _():
        for head in range(2):
            part = rotated(acc[:, head * DH:(head + 1) * DH], cosine[...], sine[...]).astype(BF)
            for block in range(2):
                out_kv[block, head, 0] = part[block * BLK:(block + 1) * BLK]

    @pl.when(step == 5)
    def _():
        for head in range(2):
            part = acc[:, head * DH:(head + 1) * DH].astype(BF)
            for block in range(2):
                out_kv[block, head, 0] = part[block * BLK:(block + 1) * BLK]


def project_both(x0, x1, w, down, up, cosine, sine):
    width = x0.shape[1]
    rank = down.shape[1]
    return pl.pallas_call(
        both_kernel,
        grid=(6,),
        in_specs=[
            whole((BLK, width)),
            whole((BLK, width)),
            pl.BlockSpec((width, 2 * DH), lambda j: (0, j)),
            whole(down.shape),
            pl.BlockSpec((rank, 2 * DH), lambda j: (0, j)),
            whole((2 * BLK, DH)),
            whole((2 * BLK, DH)),
        ],
        out_specs=[
            pl.BlockSpec((2, 2, BLK, DH), lambda j: (0, jnp.minimum(j, 3), 0, 0)),
            pl.BlockSpec((2, 2, 1, BLK, DH), lambda j: (0, 0, jnp.maximum(j - 4, 0), 0, 0)),
        ],
        out_shape=[
            jax.ShapeDtypeStruct((2, 8, BLK, DH), BF),
            jax.ShapeDtypeStruct((2, 2, 2, BLK, DH), BF),
        ],
        scratch_shapes=[pltpu.VMEM((2 * BLK, rank), BF), pltpu.VMEM((2 * BLK, width), BF)],
        compiler_params=pltpu.CompilerParams(vmem_limit_bytes=40 * 2**20),
        cost_estimate=pl.CostEstimate(
            flops=2 * 2 * BLK * width * 12 * DH, bytes_accessed=width * 12 * DH * 2, transcendentals=0
        ),
        name="project_both",
    )(x0, x1, w, down, up, cosine, sine)


def whole(shape):
    return pl.BlockSpec(shape, lambda *_: (0,) * len(shape))


def project(for_keys, x0, x1, w, low, up, cosine, sine):
    width = x0.shape[1]
    rank = low.shape[1]
    makes_mid = low.shape[0] == width
    steps, base = (2, 4) if for_keys else (4, 0)
    if for_keys:
        out_spec = pl.BlockSpec((2, 2, 1, BLK, DH), lambda j: (0, 0, j, 0, 0))
        out_shape = jax.ShapeDtypeStruct((2, 2, 2, BLK, DH), BF)
    else:
        out_spec = pl.BlockSpec((2, 2, BLK, DH), lambda j: (0, j, 0, 0))
        out_shape = jax.ShapeDtypeStruct((2, 8, BLK, DH), BF)
    mid_spec, mid_shape = [], []
    if makes_mid:
        mid_spec, mid_shape = [whole((2 * BLK, rank))], [jax.ShapeDtypeStruct((2 * BLK, rank), BF)]
    made = pl.pallas_call(
        functools.partial(kv_kernel if for_keys else q_kernel, makes_mid),
        grid=(steps,),
        in_specs=[
            whole((BLK, width)),
            whole((BLK, width)),
            pl.BlockSpec((width, 2 * DH), lambda j: (0, base + j)),
            whole(low.shape),
            pl.BlockSpec((rank, 2 * DH), lambda j: (0, base + j)),
            whole((2 * BLK, DH)),
            whole((2 * BLK, DH)),
        ],
        out_specs=[out_spec] + mid_spec,
        out_shape=[out_shape] + mid_shape,
        scratch_shapes=[pltpu.VMEM((2 * BLK, width), BF)],
        compiler_params=pltpu.CompilerParams(vmem_limit_bytes=40 * 2**20),
        cost_estimate=pl.CostEstimate(
            flops=2 * 2 * BLK * width * 2 * DH * steps, bytes_accessed=width * 2 * DH * steps * 2, transcendentals=0
        ),
        name="project_kv" if for_keys else "project_q",
    )(x0, x1, w, low, up, cosine, sine)
    return made if makes_mid else made[0]


def sort_kernel(source, a, b, c, d, out):
    for slot in range(H):
        pick = source[slot]
        which = pick // 8
        inner = pick % 8
        for k, ref in enumerate((a, b, c, d)):

            @pl.when(which == k)
            def _(ref=ref):
                out[slot // 4, slot % 4] = ref[inner]


def sort_heads(source, parts):
    return pl.pallas_call(
        sort_kernel,
        in_specs=[pl.BlockSpec(memory_space=pltpu.SMEM)] + [pl.BlockSpec(memory_space=pltpu.VMEM)] * 4,
        out_specs=pl.BlockSpec(memory_space=pltpu.VMEM),
        out_shape=jax.ShapeDtypeStruct((KV, 4, BLK, DH), BF),
        compiler_params=pltpu.CompilerParams(vmem_limit_bytes=16 * 2**20),
        cost_estimate=pl.CostEstimate(flops=0, bytes_accessed=2 * H * BLK * DH * 2, transcendentals=0),
        name="sort_heads",
    )(source, *parts)


def unsort_kernel(slots, a, out):
    for head in range(H):
        slot = slots[head]
        out[:, head * DH:(head + 1) * DH] = a[slot // 4, slot % 4]


def unsort_heads(slots, a):
    return pl.pallas_call(
        unsort_kernel,
        in_specs=[pl.BlockSpec(memory_space=pltpu.SMEM), pl.BlockSpec(memory_space=pltpu.VMEM)],
        out_specs=pl.BlockSpec(memory_space=pltpu.VMEM),
        out_shape=jax.ShapeDtypeStruct((BLK, H * DH), BF),
        compiler_params=pltpu.CompilerParams(vmem_limit_bytes=16 * 2**20),
        cost_estimate=pl.CostEstimate(flops=0, bytes_accessed=2 * H * BLK * DH * 2, transcendentals=0),
        name="unsort_heads",
    )(slots, a)


def attend_kernel(blocks, starts, own, q_ref, kv0, kv1, out, pairs, sems, top, total, acc, floor):
    yh = own[0]

    def copies_of(z):
        row = (own[1] - z + NZ) % NZ
        return [
            pltpu.make_async_copy(src.at[:, pl.ds(row, 1)], pairs.at[stage, :, pl.ds(z, 1)], sems.at[2 * z + stage])
            for stage, src in enumerate((kv0, kv1))
        ]

    for z in range(NZ):
        for copy in copies_of(z):
            copy.start()

    def gathered(begin_block, width, kind):
        parts = []
        for k in range(width):
            key_block = jnp.maximum(begin_block + k, 0)
            low = (key_block // (NC * NYH * NX)) % NYL
            stage = ((key_block // NC) % NYH) ^ yh
            source = (((key_block // (NC * NYH)) % NX) * NYL + (low ^ stage)) * NC + key_block % NC
            parts.append(pairs[stage, source, key_block // (NC * NYH * NX * NYL), kind])
        return jnp.concatenate(parts, axis=0)

    def one_tile(tile):
        rows = 4 * BLK
        block = blocks[tile]
        first = block * BLK

        def start_of(place):
            found = jnp.int32(0)
            for d in range(1, DOCS):
                found = jnp.maximum(found, jnp.where(starts[d] <= place, starts[d], 0))
            return found

        span = block + 1 - start_of(first) // BLK
        latest_start = start_of(first + BLK - 1)
        factor = (DH ** -0.5) * 1.4426950408889634

        top[...] = jnp.full(top.shape, NEG_BIG, F32)
        total[...] = jnp.zeros(total.shape, F32)
        acc[...] = jnp.zeros(acc.shape, F32)
        q = q_ref[tile].reshape(rows, DH)

        place = first + lax.broadcasted_iota(jnp.int32, (rows, DH), 0) % BLK
        begin = jnp.zeros((rows, DH), jnp.int32)
        for d in range(1, DOCS):
            begin = jnp.maximum(begin, jnp.where(place >= starts[d], starts[d], 0))
        floor[...] = begin

        def step(begin_block, width, at_end, at_start):
            k_tile = gathered(begin_block, width, 0)
            v_tile = gathered(begin_block, width, 1)
            scores = lax.dot_general(q, k_tile, (((1,), (1,)), ((), ())), preferred_element_type=F32)
            parts = [scores[:, j:j + DH] * factor for j in range(0, width * BLK, DH)]
            lane = lax.broadcasted_iota(jnp.int32, (rows, DH), 1)
            if at_start:
                lowest = floor[...] - lane
                parts = [jnp.where(lowest <= (begin_block + j) * BLK, part, -jnp.inf) for j, part in enumerate(parts)]
            if at_end:
                inside = lane <= lax.broadcasted_iota(jnp.int32, (rows, DH), 0) % BLK
                parts[-1] = jnp.where(inside, parts[-1], -jnp.inf)
            old = top[...]
            peak = functools.reduce(jnp.maximum, parts)
            new = jnp.maximum(old, jnp.max(peak, axis=1, keepdims=True))
            shrink = jnp.exp2(old - new)
            powers = [jnp.exp2(part - new) for part in parts]
            top[...] = new
            total[...] = total[...] * shrink + functools.reduce(jnp.add, powers)
            weights = jnp.concatenate([p.astype(BF) for p in powers], axis=1)
            acc[...] = acc[...] * shrink + jnp.dot(weights, v_tile, preferred_element_type=F32)

        whole_steps = (span + WIDE // 2 - 1) // WIDE

        def starting(begin_block):
            return begin_block * BLK < latest_start

        def either(begin_block, width, at_end):
            early = starting(begin_block)

            @pl.when(early)
            def _():
                step(begin_block, width, at_end, True)

            @pl.when(jnp.logical_not(early))
            def _():
                step(begin_block, width, at_end, False)

        @pl.when(whole_steps > 0)
        def _():
            either(block + 1 - WIDE, WIDE, True)

        def body(index, carry):
            either(block + 1 - WIDE * (index + 1), WIDE, False)
            return carry

        lax.fori_loop(1, whole_steps, body, 0)

        left = span - WIDE * whole_steps

        @pl.when((left > 0) & (whole_steps == 0))
        def _():
            step(block + 1 - WIDE // 2, WIDE // 2, True, True)

        @pl.when((left > 0) & (whole_steps > 0))
        def _():
            step(block + 1 - WIDE * whole_steps - WIDE // 2, WIDE // 2, False, True)

        out[tile] = (acc[...] / jnp.sum(total[...], axis=1, keepdims=True)).astype(BF).reshape(4, BLK, DH)

    def pair(z, carry):
        for copy in copies_of(z):
            copy.wait()
        one_tile(2 * z)
        one_tile(2 * z + 1)
        return carry

    lax.fori_loop(0, NZ, pair, 0)


def attend(blocks, starts, own, q, kv0, kv1):
    rows = 4 * BLK
    return pl.pallas_call(
        attend_kernel,
        in_specs=[pl.BlockSpec(memory_space=pltpu.SMEM)] * 3
        + [
            pl.BlockSpec(memory_space=pltpu.VMEM),
            pl.BlockSpec(memory_space=pl.ANY),
            pl.BlockSpec(memory_space=pl.ANY),
        ],
        out_specs=pl.BlockSpec(memory_space=pltpu.VMEM),
        out_shape=jax.ShapeDtypeStruct((8, 4, BLK, DH), BF),
        scratch_shapes=[
            pltpu.VMEM((2, NX * NYL * NC, NZ, 2, BLK, DH), BF),
            pltpu.SemaphoreType.DMA((2 * NZ,)),
            pltpu.VMEM((rows, DH), F32),
            pltpu.VMEM((rows, DH), F32),
            pltpu.VMEM((rows, DH), F32),
            pltpu.VMEM((rows, DH), jnp.int32),
        ],
        compiler_params=pltpu.CompilerParams(vmem_limit_bytes=60 * 2**20),
        cost_estimate=pl.CostEstimate(flops=10**10, bytes_accessed=10 * 2**20, transcendentals=10**7),
        name="attend",
    )(blocks, starts, own, q, kv0, kv1)


def per_device(tokens, w, down, up, document_index, query_to_key_head):
    z, yl, x, yh, c = (lax.axis_index(a) for a in ALL)
    block = flat(z, yl, x, yh, c)
    far_block = flat(z, 1 - yl, x, 1 - yh, c)
    other = 1 - 2 * c

    far = lax.ppermute(tokens, ALL, CROSS)
    near_pair = lax.ppermute(tokens, "c", SWAP)

    near_cos, near_sin = rope_tables(jnp.stack([block, block + other]))
    far_cos, far_sin = rope_tables(jnp.stack([far_block, far_block + other]))

    def split_kv(part, beside=None):
        mine, theirs = part[0], lax.ppermute(part[1], "c", SWAP)
        heads = jnp.where(c == 0, jnp.concatenate([mine, theirs], 0), jnp.concatenate([theirs, mine], 0))
        rows = []
        for k in range(NZ):
            head = lax.dynamic_index_in_dim(heads, (z + k) % NZ, 0, keepdims=False)
            rows.append(lax.ppermute(head, "z", [(i, (i + k) % NZ) for i in range(NZ)]) if k else head)
        if beside is not None:
            rows, _ = lax.optimization_barrier((rows, beside))
        return jnp.stack(rows)[None]

    q_near, kv_near = project_both(tokens, near_pair, w, down, up, near_cos, near_sin)
    far, q_near, kv_near = lax.optimization_barrier((far, q_near, kv_near))
    far_pair = lax.ppermute(far, "c", SWAP)
    q_far, mid_far = project(False, far, far_pair, w, down, up, far_cos, far_sin)
    rows_near = split_kv(kv_near, mid_far)
    kv0 = lax.all_gather(rows_near, ("x", "yl", "c"), axis=0, tiled=True)
    mid_far, _ = lax.optimization_barrier((mid_far, rows_near))
    home_c = lax.ppermute(q_far[0], ALL, CROSS)
    home_d = lax.ppermute(q_far[1], ALL, CROSS_OTHER)
    kv_far = project(True, far, far_pair, w, mid_far, up, far_cos, far_sin)
    kv_far, home_c = lax.optimization_barrier((kv_far, home_c))
    rows_far, home_d = lax.optimization_barrier((split_kv(kv_far), home_d))
    kv1 = lax.all_gather(rows_far, ("x", "yl", "c"), axis=0, tiled=True)

    parts = (
        q_near[0],
        lax.ppermute(q_near[1], "c", SWAP),
        home_c,
        home_d,
    )
    member = (query_to_key_head % 4) * 2 + query_to_key_head // 4
    heads = jnp.arange(H, dtype=jnp.int32)
    same = (member[None, :] == member[:, None]) & (heads[None, :] < heads[:, None])
    slots = member * 4 + jnp.sum(same.astype(jnp.int32), axis=1)
    source_of_head = ((heads // 8) ^ (yh * 2 + c)) * 8 + heads % 8
    source = jnp.sum(jnp.where(slots[None, :] == heads[:, None], source_of_head[None, :], 0), axis=1)
    sorted_q = sort_heads(source, parts)
    q = lax.all_to_all(sorted_q, ALL, split_axis=0, concat_axis=0, tiled=True, axis_index_groups=GROUPS)

    member_z = jnp.arange(8, dtype=jnp.int32) // 2
    member_yh = jnp.arange(8, dtype=jnp.int32) % 2
    blocks = flat(member_z, (yl ^ yh) ^ member_yh, (x - z + member_z) % NX, member_yh, c).astype(jnp.int32)
    starts = jnp.sum(
        (document_index[None, :] < jnp.arange(DOCS, dtype=jnp.int32)[:, None]).astype(jnp.int32), axis=1
    )
    context = attend(blocks, starts, jnp.stack([yh, z]).astype(jnp.int32), q, kv0, kv1)
    home = lax.all_to_all(context, ALL, split_axis=0, concat_axis=0, tiled=True, axis_index_groups=GROUPS)
    return unsort_heads(slots, home)


def solution(mesh):
    fine = Mesh(mesh.devices.reshape(NZ, NYL, NX, NYH, NC), ALL)
    return jax.shard_map(
        per_device,
        mesh=fine,
        in_specs=(P(ALL, None), P(None, ("yh", "c")), P(), P(None, ("yh", "c")), P(), P()),
        out_specs=P(ALL, None),
        check_vma=False,
    )
```

```python
import functools

import jax
import jax.numpy as jnp
from jax import lax
from jax.experimental import pallas as pl
from jax.experimental.pallas import tpu as pltpu
from jax.sharding import Mesh
from jax.sharding import PartitionSpec as P

H = 32
KV = 8
DH = 128
BLK = 128
THETA = 500000.0
ADAPTER_SCALE = 0.5
NEG_BIG = -1e30
DOCS = 4

NZ, NYL, NX, NYH, NC = 4, 2, 4, 2, 2
ALL = ("z", "yl", "x", "yh", "c")
BF = jnp.bfloat16
F32 = jnp.float32
WIDE = 8


def flat(z, yl, x, yh, c):
    return (((z * NYL + yl) * NX + x) * NYH + yh) * NC + c


def every():
    for z in range(NZ):
        for yl in range(NYL):
            for x in range(NX):
                for yh in range(NYH):
                    for c in range(NC):
                        yield z, yl, x, yh, c


CROSS = [(flat(*d), flat(d[0], 1 - d[1], d[2], 1 - d[3], d[4])) for d in every()]
CROSS_OTHER = [(flat(*d), flat(d[0], 1 - d[1], d[2], 1 - d[3], 1 - d[4])) for d in every()]
SWAP = [(0, 1), (1, 0)]
GROUPS = [
    [flat(z, yl0 ^ yh, (x0 + z) % NX, yh, c) for z in range(NZ) for yh in range(NYH)]
    for x0 in range(NX)
    for yl0 in range(NYL)
    for c in range(NC)
]


def rope_tables(blocks):
    half = DH // 2
    frequency = THETA ** (-(jnp.arange(half, dtype=F32) * 2.0) / DH)
    places = (blocks[:, None] * BLK + jnp.arange(BLK, dtype=jnp.int32)[None, :]).reshape(-1).astype(F32)
    angles = places[:, None] * frequency[None, :]
    cosine, sine = jnp.cos(angles), jnp.sin(angles)
    return jnp.concatenate([cosine, cosine], axis=1), jnp.concatenate([-sine, sine], axis=1)


def rotated(part, cosine, sine):
    return part * cosine + pltpu.roll(part, DH // 2, 1) * sine


def gather_rows(x0, x1, rows):
    rows[:BLK] = x0[...]
    rows[BLK:] = x1[...]


def kv_kernel(makes_mid, x0, x1, w, low, up, cosine, sine, out, *rest):
    step = pl.program_id(0)
    if makes_mid:
        mid, rows = rest
    else:
        mid, (rows,) = low, rest

    @pl.when(step == 0)
    def _():
        gather_rows(x0, x1, rows)
        if makes_mid:
            mid[...] = jnp.dot(rows[...], low[...], preferred_element_type=F32).astype(BF)

    acc = jnp.dot(rows[...], w[...], preferred_element_type=F32)
    acc = acc + ADAPTER_SCALE * jnp.dot(mid[...], up[...], preferred_element_type=F32)

    @pl.when(step == 0)
    def _():
        for head in range(2):
            part = rotated(acc[:, head * DH:(head + 1) * DH], cosine[...], sine[...]).astype(BF)
            for block in range(2):
                out[block, head, 0] = part[block * BLK:(block + 1) * BLK]

    @pl.when(step == 1)
    def _():
        for head in range(2):
            part = acc[:, head * DH:(head + 1) * DH].astype(BF)
            for block in range(2):
                out[block, head, 0] = part[block * BLK:(block + 1) * BLK]


def q_kernel(makes_mid, x0, x1, w, low, up, cosine, sine, out, *rest):
    step = pl.program_id(0)
    if makes_mid:
        mid, rows = rest
    else:
        mid, (rows,) = low, rest

    @pl.when(step == 0)
    def _():
        gather_rows(x0, x1, rows)
        if makes_mid:
            mid[...] = jnp.dot(rows[...], low[...], preferred_element_type=F32).astype(BF)

    acc = jnp.dot(rows[...], w[...], preferred_element_type=F32)
    acc = acc + ADAPTER_SCALE * jnp.dot(mid[...], up[...], preferred_element_type=F32)
    for head in range(2):
        part = rotated(acc[:, head * DH:(head + 1) * DH], cosine[...], sine[...]).astype(BF)
        for block in range(2):
            out[block, head] = part[block * BLK:(block + 1) * BLK]


def both_kernel(x0, x1, w, low, up, cosine, sine, out_q, out_kv, mid, rows):
    step = pl.program_id(0)

    @pl.when(step == 0)
    def _():
        gather_rows(x0, x1, rows)
        mid[...] = jnp.dot(rows[...], low[...], preferred_element_type=F32).astype(BF)

    acc = jnp.dot(rows[...], w[...], preferred_element_type=F32)
    acc = acc + ADAPTER_SCALE * jnp.dot(mid[...], up[...], preferred_element_type=F32)

    @pl.when(step < 4)
    def _():
        for head in range(2):
            part = rotated(acc[:, head * DH:(head + 1) * DH], cosine[...], sine[...]).astype(BF)
            for block in range(2):
                out_q[block, head] = part[block * BLK:(block + 1) * BLK]

    @pl.when(step == 4)
    def _():
        for head in range(2):
            part = rotated(acc[:, head * DH:(head + 1) * DH], cosine[...], sine[...]).astype(BF)
            for block in range(2):
                out_kv[block, head, 0] = part[block * BLK:(block + 1) * BLK]

    @pl.when(step == 5)
    def _():
        for head in range(2):
            part = acc[:, head * DH:(head + 1) * DH].astype(BF)
            for block in range(2):
                out_kv[block, head, 0] = part[block * BLK:(block + 1) * BLK]


def project_both(x0, x1, w, down, up, cosine, sine):
    width = x0.shape[1]
    rank = down.shape[1]
    return pl.pallas_call(
        both_kernel,
        grid=(6,),
        in_specs=[
            whole((BLK, width)),
            whole((BLK, width)),
            pl.BlockSpec((width, 2 * DH), lambda j: (0, j)),
            whole(down.shape),
            pl.BlockSpec((rank, 2 * DH), lambda j: (0, j)),
            whole((2 * BLK, DH)),
            whole((2 * BLK, DH)),
        ],
        out_specs=[
            pl.BlockSpec((2, 2, BLK, DH), lambda j: (0, jnp.minimum(j, 3), 0, 0)),
            pl.BlockSpec((2, 2, 1, BLK, DH), lambda j: (0, 0, jnp.maximum(j - 4, 0), 0, 0)),
        ],
        out_shape=[
            jax.ShapeDtypeStruct((2, 8, BLK, DH), BF),
            jax.ShapeDtypeStruct((2, 2, 2, BLK, DH), BF),
        ],
        scratch_shapes=[pltpu.VMEM((2 * BLK, rank), BF), pltpu.VMEM((2 * BLK, width), BF)],
        compiler_params=pltpu.CompilerParams(vmem_limit_bytes=40 * 2**20),
        cost_estimate=pl.CostEstimate(
            flops=2 * 2 * BLK * width * 12 * DH, bytes_accessed=width * 12 * DH * 2, transcendentals=0
        ),
        name="project_both",
    )(x0, x1, w, down, up, cosine, sine)


def whole(shape):
    return pl.BlockSpec(shape, lambda *_: (0,) * len(shape))


def project(for_keys, x0, x1, w, low, up, cosine, sine):
    width = x0.shape[1]
    rank = low.shape[1]
    makes_mid = low.shape[0] == width
    steps, base = (2, 4) if for_keys else (4, 0)
    if for_keys:
        out_spec = pl.BlockSpec((2, 2, 1, BLK, DH), lambda j: (0, 0, j, 0, 0))
        out_shape = jax.ShapeDtypeStruct((2, 2, 2, BLK, DH), BF)
    else:
        out_spec = pl.BlockSpec((2, 2, BLK, DH), lambda j: (0, j, 0, 0))
        out_shape = jax.ShapeDtypeStruct((2, 8, BLK, DH), BF)
    mid_spec, mid_shape = [], []
    if makes_mid:
        mid_spec, mid_shape = [whole((2 * BLK, rank))], [jax.ShapeDtypeStruct((2 * BLK, rank), BF)]
    made = pl.pallas_call(
        functools.partial(kv_kernel if for_keys else q_kernel, makes_mid),
        grid=(steps,),
        in_specs=[
            whole((BLK, width)),
            whole((BLK, width)),
            pl.BlockSpec((width, 2 * DH), lambda j: (0, base + j)),
            whole(low.shape),
            pl.BlockSpec((rank, 2 * DH), lambda j: (0, base + j)),
            whole((2 * BLK, DH)),
            whole((2 * BLK, DH)),
        ],
        out_specs=[out_spec] + mid_spec,
        out_shape=[out_shape] + mid_shape,
        scratch_shapes=[pltpu.VMEM((2 * BLK, width), BF)],
        compiler_params=pltpu.CompilerParams(vmem_limit_bytes=40 * 2**20),
        cost_estimate=pl.CostEstimate(
            flops=2 * 2 * BLK * width * 2 * DH * steps, bytes_accessed=width * 2 * DH * steps * 2, transcendentals=0
        ),
        name="project_kv" if for_keys else "project_q",
    )(x0, x1, w, low, up, cosine, sine)
    return made if makes_mid else made[0]


def sort_kernel(source, a, b, c, d, out):
    for slot in range(H):
        pick = source[slot]
        which = pick // 8
        inner = pick % 8
        for k, ref in enumerate((a, b, c, d)):

            @pl.when(which == k)
            def _(ref=ref):
                out[slot // 4, slot % 4] = ref[inner]


def sort_heads(source, parts):
    return pl.pallas_call(
        sort_kernel,
        in_specs=[pl.BlockSpec(memory_space=pltpu.SMEM)] + [pl.BlockSpec(memory_space=pltpu.VMEM)] * 4,
        out_specs=pl.BlockSpec(memory_space=pltpu.VMEM),
        out_shape=jax.ShapeDtypeStruct((KV, 4, BLK, DH), BF),
        compiler_params=pltpu.CompilerParams(vmem_limit_bytes=16 * 2**20),
        cost_estimate=pl.CostEstimate(flops=0, bytes_accessed=2 * H * BLK * DH * 2, transcendentals=0),
        name="sort_heads",
    )(source, *parts)


def unsort_kernel(slots, a, out):
    for head in range(H):
        slot = slots[head]
        out[:, head * DH:(head + 1) * DH] = a[slot // 4, slot % 4]


def unsort_heads(slots, a):
    return pl.pallas_call(
        unsort_kernel,
        in_specs=[pl.BlockSpec(memory_space=pltpu.SMEM), pl.BlockSpec(memory_space=pltpu.VMEM)],
        out_specs=pl.BlockSpec(memory_space=pltpu.VMEM),
        out_shape=jax.ShapeDtypeStruct((BLK, H * DH), BF),
        compiler_params=pltpu.CompilerParams(vmem_limit_bytes=16 * 2**20),
        cost_estimate=pl.CostEstimate(flops=0, bytes_accessed=2 * H * BLK * DH * 2, transcendentals=0),
        name="unsort_heads",
    )(slots, a)


def attend_kernel(blocks, starts, own, q_ref, kv, out, pairs, sems, top, total, acc, floor):
    yh = own[0]

    def copy_of(z):
        return pltpu.make_async_copy(
            kv.at[:, pl.ds((own[1] - z + NZ) % NZ, 1)], pairs.at[:, pl.ds(z, 1)], sems.at[z]
        )

    for z in range(NZ):
        copy_of(z).start()

    def gathered(begin_block, width, kind):
        parts = []
        for k in range(width):
            key_block = jnp.maximum(begin_block + k, 0)
            low = (key_block // (NC * NYH * NX)) % NYL
            stage = ((key_block // NC) % NYH) ^ yh
            source = (((key_block // (NC * NYH)) % NX) * NYL + (low ^ stage)) * NC + key_block % NC
            parts.append(pairs[source, key_block // (NC * NYH * NX * NYL), stage, kind])
        return jnp.concatenate(parts, axis=0)

    def one_tile(tile):
        rows = 4 * BLK
        block = blocks[tile]
        first = block * BLK

        def start_of(place):
            found = jnp.int32(0)
            for d in range(1, DOCS):
                found = jnp.maximum(found, jnp.where(starts[d] <= place, starts[d], 0))
            return found

        span = block + 1 - start_of(first) // BLK
        latest_start = start_of(first + BLK - 1)
        factor = (DH ** -0.5) * 1.4426950408889634

        top[...] = jnp.full(top.shape, NEG_BIG, F32)
        total[...] = jnp.zeros(total.shape, F32)
        acc[...] = jnp.zeros(acc.shape, F32)
        q = q_ref[tile].reshape(rows, DH)

        place = first + lax.broadcasted_iota(jnp.int32, (rows, DH), 0) % BLK
        begin = jnp.zeros((rows, DH), jnp.int32)
        for d in range(1, DOCS):
            begin = jnp.maximum(begin, jnp.where(place >= starts[d], starts[d], 0))
        floor[...] = begin

        def step(begin_block, width, at_end, at_start):
            k_tile = gathered(begin_block, width, 0)
            v_tile = gathered(begin_block, width, 1)
            scores = lax.dot_general(q, k_tile, (((1,), (1,)), ((), ())), preferred_element_type=F32)
            parts = [scores[:, j:j + DH] * factor for j in range(0, width * BLK, DH)]
            lane = lax.broadcasted_iota(jnp.int32, (rows, DH), 1)
            if at_start:
                lowest = floor[...] - lane
                parts = [jnp.where(lowest <= (begin_block + j) * BLK, part, -jnp.inf) for j, part in enumerate(parts)]
            if at_end:
                inside = lane <= lax.broadcasted_iota(jnp.int32, (rows, DH), 0) % BLK
                parts[-1] = jnp.where(inside, parts[-1], -jnp.inf)
            old = top[...]
            peak = functools.reduce(jnp.maximum, parts)
            new = jnp.maximum(old, jnp.max(peak, axis=1, keepdims=True))
            shrink = jnp.exp2(old - new)
            powers = [jnp.exp2(part - new) for part in parts]
            top[...] = new
            total[...] = total[...] * shrink + functools.reduce(jnp.add, powers)
            weights = jnp.concatenate([p.astype(BF) for p in powers], axis=1)
            acc[...] = acc[...] * shrink + jnp.dot(weights, v_tile, preferred_element_type=F32)

        whole_steps = (span + WIDE // 2 - 1) // WIDE

        def starting(begin_block):
            return begin_block * BLK < latest_start

        def either(begin_block, width, at_end):
            early = starting(begin_block)

            @pl.when(early)
            def _():
                step(begin_block, width, at_end, True)

            @pl.when(jnp.logical_not(early))
            def _():
                step(begin_block, width, at_end, False)

        @pl.when(whole_steps > 0)
        def _():
            either(block + 1 - WIDE, WIDE, True)

        def body(index, carry):
            either(block + 1 - WIDE * (index + 1), WIDE, False)
            return carry

        lax.fori_loop(1, whole_steps, body, 0)

        left = span - WIDE * whole_steps

        @pl.when((left > 0) & (whole_steps == 0))
        def _():
            step(block + 1 - WIDE // 2, WIDE // 2, True, True)

        @pl.when((left > 0) & (whole_steps > 0))
        def _():
            step(block + 1 - WIDE * whole_steps - WIDE // 2, WIDE // 2, False, True)

        out[tile] = (acc[...] / jnp.sum(total[...], axis=1, keepdims=True)).astype(BF).reshape(4, BLK, DH)

    def pair(z, carry):
        copy_of(z).wait()
        one_tile(2 * z)
        one_tile(2 * z + 1)
        return carry

    lax.fori_loop(0, NZ, pair, 0)


def attend(blocks, starts, own, q, kv):
    rows = 4 * BLK
    return pl.pallas_call(
        attend_kernel,
        in_specs=[pl.BlockSpec(memory_space=pltpu.SMEM)] * 3
        + [
            pl.BlockSpec(memory_space=pltpu.VMEM),
            pl.BlockSpec(memory_space=pl.ANY),
        ],
        out_specs=pl.BlockSpec(memory_space=pltpu.VMEM),
        out_shape=jax.ShapeDtypeStruct((8, 4, BLK, DH), BF),
        scratch_shapes=[
            pltpu.VMEM((NX * NYL * NC, NZ, 2, 2, BLK, DH), BF),
            pltpu.SemaphoreType.DMA((NZ,)),
            pltpu.VMEM((rows, DH), F32),
            pltpu.VMEM((rows, DH), F32),
            pltpu.VMEM((rows, DH), F32),
            pltpu.VMEM((rows, DH), jnp.int32),
        ],
        compiler_params=pltpu.CompilerParams(vmem_limit_bytes=60 * 2**20),
        cost_estimate=pl.CostEstimate(flops=10**10, bytes_accessed=10 * 2**20, transcendentals=10**7),
        name="attend",
    )(blocks, starts, own, q, kv)


def per_device(tokens, w, down, up, document_index, query_to_key_head):
    z, yl, x, yh, c = (lax.axis_index(a) for a in ALL)
    block = flat(z, yl, x, yh, c)
    far_block = flat(z, 1 - yl, x, 1 - yh, c)
    other = 1 - 2 * c

    far = lax.ppermute(tokens, ALL, CROSS)
    near_pair = lax.ppermute(tokens, "c", SWAP)

    near_cos, near_sin = rope_tables(jnp.stack([block, block + other]))
    far_cos, far_sin = rope_tables(jnp.stack([far_block, far_block + other]))

    def split_kv(near, far, beside):
        mine, theirs = jnp.stack([near[0], far[0]], 1), lax.ppermute(jnp.stack([near[1], far[1]], 1), "c", SWAP)
        heads = jnp.where(c == 0, jnp.concatenate([mine, theirs], 0), jnp.concatenate([theirs, mine], 0))
        rows = []
        for k in range(NZ):
            head = lax.dynamic_index_in_dim(heads, (z + k) % NZ, 0, keepdims=False)
            rows.append(lax.ppermute(head, "z", [(i, (i + k) % NZ) for i in range(NZ)]) if k else head)
        rows, beside = lax.optimization_barrier((rows, beside))
        return jnp.stack(rows)[None], beside

    q_near, kv_near = project_both(tokens, near_pair, w, down, up, near_cos, near_sin)
    far, q_near, kv_near = lax.optimization_barrier((far, q_near, kv_near))
    far_pair = lax.ppermute(far, "c", SWAP)
    kv_far, mid_far = project(True, far, far_pair, w, down, up, far_cos, far_sin)
    q_far = project(False, far, far_pair, w, mid_far, up, far_cos, far_sin)
    rows, q_far = split_kv(kv_near, kv_far, q_far)
    kv = lax.all_gather(rows, ("x", "yl", "c"), axis=0, tiled=True)
    home_c = lax.ppermute(q_far[0], ALL, CROSS)
    home_d = lax.ppermute(q_far[1], ALL, CROSS_OTHER)

    parts = (
        q_near[0],
        lax.ppermute(q_near[1], "c", SWAP),
        home_c,
        home_d,
    )
    member = (query_to_key_head % 4) * 2 + query_to_key_head // 4
    heads = jnp.arange(H, dtype=jnp.int32)
    same = (member[None, :] == member[:, None]) & (heads[None, :] < heads[:, None])
    slots = member * 4 + jnp.sum(same.astype(jnp.int32), axis=1)
    source_of_head = ((heads // 8) ^ (yh * 2 + c)) * 8 + heads % 8
    source = jnp.sum(jnp.where(slots[None, :] == heads[:, None], source_of_head[None, :], 0), axis=1)
    sorted_q = sort_heads(source, parts)
    q = lax.all_to_all(sorted_q, ALL, split_axis=0, concat_axis=0, tiled=True, axis_index_groups=GROUPS)

    member_z = jnp.arange(8, dtype=jnp.int32) // 2
    member_yh = jnp.arange(8, dtype=jnp.int32) % 2
    blocks = flat(member_z, (yl ^ yh) ^ member_yh, (x - z + member_z) % NX, member_yh, c).astype(jnp.int32)
    starts = jnp.sum(
        (document_index[None, :] < jnp.arange(DOCS, dtype=jnp.int32)[:, None]).astype(jnp.int32), axis=1
    )
    context = attend(blocks, starts, jnp.stack([yh, z]).astype(jnp.int32), q, kv)
    home = lax.all_to_all(context, ALL, split_axis=0, concat_axis=0, tiled=True, axis_index_groups=GROUPS)
    return unsort_heads(slots, home)


def solution(mesh):
    fine = Mesh(mesh.devices.reshape(NZ, NYL, NX, NYH, NC), ALL)
    return jax.shard_map(
        per_device,
        mesh=fine,
        in_specs=(P(ALL, None), P(None, ("yh", "c")), P(), P(None, ("yh", "c")), P(), P()),
        out_specs=P(ALL, None),
        check_vma=False,
    )
```

```python
import functools

import jax
import jax.numpy as jnp
from jax import lax
from jax.experimental import pallas as pl
from jax.experimental.pallas import tpu as pltpu
from jax.sharding import Mesh
from jax.sharding import PartitionSpec as P

H = 32
KV = 8
DH = 128
BLK = 128
THETA = 500000.0
ADAPTER_SCALE = 0.5
NEG_BIG = -1e30
DOCS = 4

NZ, NYL, NX, NYH, NC = 4, 2, 4, 2, 2
ALL = ("z", "yl", "x", "yh", "c")
BF = jnp.bfloat16
F32 = jnp.float32
WIDE = 16
TAIL = 4


def flat(z, yl, x, yh, c):
    return (((z * NYL + yl) * NX + x) * NYH + yh) * NC + c


def every():
    for z in range(NZ):
        for yl in range(NYL):
            for x in range(NX):
                for yh in range(NYH):
                    for c in range(NC):
                        yield z, yl, x, yh, c


CROSS = [(flat(*d), flat(d[0], 1 - d[1], d[2], 1 - d[3], d[4])) for d in every()]
CROSS_OTHER = [(flat(*d), flat(d[0], 1 - d[1], d[2], 1 - d[3], 1 - d[4])) for d in every()]
SWAP = [(0, 1), (1, 0)]
GROUPS = [
    [flat(z, yl0 ^ yh, (x0 + z) % NX, yh, c) for z in range(NZ) for yh in range(NYH)]
    for x0 in range(NX)
    for yl0 in range(NYL)
    for c in range(NC)
]


def rope_tables(blocks):
    half = DH // 2
    frequency = THETA ** (-(jnp.arange(half, dtype=F32) * 2.0) / DH)
    places = (blocks[:, None] * BLK + jnp.arange(BLK, dtype=jnp.int32)[None, :]).reshape(-1).astype(F32)
    angles = places[:, None] * frequency[None, :]
    cosine, sine = jnp.cos(angles), jnp.sin(angles)
    return jnp.concatenate([cosine, cosine], axis=1), jnp.concatenate([-sine, sine], axis=1)


def rotated(part, cosine, sine):
    return part * cosine + pltpu.roll(part, DH // 2, 1) * sine


def gather_rows(x0, x1, rows):
    rows[:BLK] = x0[...]
    rows[BLK:] = x1[...]


def kv_kernel(makes_mid, x0, x1, w, low, up, cosine, sine, out, *rest):
    step = pl.program_id(0)
    if makes_mid:
        mid, rows = rest
    else:
        mid, (rows,) = low, rest

    @pl.when(step == 0)
    def _():
        gather_rows(x0, x1, rows)
        if makes_mid:
            mid[...] = jnp.dot(rows[...], low[...], preferred_element_type=F32).astype(BF)

    acc = jnp.dot(rows[...], w[...], preferred_element_type=F32)
    acc = acc + ADAPTER_SCALE * jnp.dot(mid[...], up[...], preferred_element_type=F32)

    @pl.when(step == 0)
    def _():
        for head in range(2):
            part = rotated(acc[:, head * DH:(head + 1) * DH], cosine[...], sine[...]).astype(BF)
            for block in range(2):
                out[block, head, 0] = part[block * BLK:(block + 1) * BLK]

    @pl.when(step == 1)
    def _():
        for head in range(2):
            part = acc[:, head * DH:(head + 1) * DH].astype(BF)
            for block in range(2):
                out[block, head, 0] = part[block * BLK:(block + 1) * BLK]


def q_kernel(makes_mid, x0, x1, w, low, up, cosine, sine, out, *rest):
    step = pl.program_id(0)
    if makes_mid:
        mid, rows = rest
    else:
        mid, (rows,) = low, rest

    @pl.when(step == 0)
    def _():
        gather_rows(x0, x1, rows)
        if makes_mid:
            mid[...] = jnp.dot(rows[...], low[...], preferred_element_type=F32).astype(BF)

    acc = jnp.dot(rows[...], w[...], preferred_element_type=F32)
    acc = acc + ADAPTER_SCALE * jnp.dot(mid[...], up[...], preferred_element_type=F32)
    for head in range(2):
        part = rotated(acc[:, head * DH:(head + 1) * DH], cosine[...], sine[...]).astype(BF)
        for block in range(2):
            out[block, head] = part[block * BLK:(block + 1) * BLK]


def both_kernel(x0, x1, w, low, up, cosine, sine, out_q, out_kv, mid, rows):
    step = pl.program_id(0)

    @pl.when(step == 0)
    def _():
        gather_rows(x0, x1, rows)
        mid[...] = jnp.dot(rows[...], low[...], preferred_element_type=F32).astype(BF)

    acc = jnp.dot(rows[...], w[...], preferred_element_type=F32)
    acc = acc + ADAPTER_SCALE * jnp.dot(mid[...], up[...], preferred_element_type=F32)

    @pl.when(step < 4)
    def _():
        for head in range(2):
            part = rotated(acc[:, head * DH:(head + 1) * DH], cosine[...], sine[...]).astype(BF)
            for block in range(2):
                out_q[block, head] = part[block * BLK:(block + 1) * BLK]

    @pl.when(step == 4)
    def _():
        for head in range(2):
            part = rotated(acc[:, head * DH:(head + 1) * DH], cosine[...], sine[...]).astype(BF)
            for block in range(2):
                out_kv[block, head, 0] = part[block * BLK:(block + 1) * BLK]

    @pl.when(step == 5)
    def _():
        for head in range(2):
            part = acc[:, head * DH:(head + 1) * DH].astype(BF)
            for block in range(2):
                out_kv[block, head, 0] = part[block * BLK:(block + 1) * BLK]


def project_both(x0, x1, w, down, up, cosine, sine):
    width = x0.shape[1]
    rank = down.shape[1]
    return pl.pallas_call(
        both_kernel,
        grid=(6,),
        in_specs=[
            whole((BLK, width)),
            whole((BLK, width)),
            pl.BlockSpec((width, 2 * DH), lambda j: (0, j)),
            whole(down.shape),
            pl.BlockSpec((rank, 2 * DH), lambda j: (0, j)),
            whole((2 * BLK, DH)),
            whole((2 * BLK, DH)),
        ],
        out_specs=[
            pl.BlockSpec((2, 2, BLK, DH), lambda j: (0, jnp.minimum(j, 3), 0, 0)),
            pl.BlockSpec((2, 2, 1, BLK, DH), lambda j: (0, 0, jnp.maximum(j - 4, 0), 0, 0)),
        ],
        out_shape=[
            jax.ShapeDtypeStruct((2, 8, BLK, DH), BF),
            jax.ShapeDtypeStruct((2, 2, 2, BLK, DH), BF),
        ],
        scratch_shapes=[pltpu.VMEM((2 * BLK, rank), BF), pltpu.VMEM((2 * BLK, width), BF)],
        compiler_params=pltpu.CompilerParams(vmem_limit_bytes=40 * 2**20),
        cost_estimate=pl.CostEstimate(
            flops=2 * 2 * BLK * width * 12 * DH, bytes_accessed=width * 12 * DH * 2, transcendentals=0
        ),
        name="project_both",
    )(x0, x1, w, down, up, cosine, sine)


def whole(shape):
    return pl.BlockSpec(shape, lambda *_: (0,) * len(shape))


def project(for_keys, x0, x1, w, low, up, cosine, sine):
    width = x0.shape[1]
    rank = low.shape[1]
    makes_mid = low.shape[0] == width
    steps, base = (2, 4) if for_keys else (4, 0)
    if for_keys:
        out_spec = pl.BlockSpec((2, 2, 1, BLK, DH), lambda j: (0, 0, j, 0, 0))
        out_shape = jax.ShapeDtypeStruct((2, 2, 2, BLK, DH), BF)
    else:
        out_spec = pl.BlockSpec((2, 2, BLK, DH), lambda j: (0, j, 0, 0))
        out_shape = jax.ShapeDtypeStruct((2, 8, BLK, DH), BF)
    mid_spec, mid_shape = [], []
    if makes_mid:
        mid_spec, mid_shape = [whole((2 * BLK, rank))], [jax.ShapeDtypeStruct((2 * BLK, rank), BF)]
    made = pl.pallas_call(
        functools.partial(kv_kernel if for_keys else q_kernel, makes_mid),
        grid=(steps,),
        in_specs=[
            whole((BLK, width)),
            whole((BLK, width)),
            pl.BlockSpec((width, 2 * DH), lambda j: (0, base + j)),
            whole(low.shape),
            pl.BlockSpec((rank, 2 * DH), lambda j: (0, base + j)),
            whole((2 * BLK, DH)),
            whole((2 * BLK, DH)),
        ],
        out_specs=[out_spec] + mid_spec,
        out_shape=[out_shape] + mid_shape,
        scratch_shapes=[pltpu.VMEM((2 * BLK, width), BF)],
        compiler_params=pltpu.CompilerParams(vmem_limit_bytes=40 * 2**20),
        cost_estimate=pl.CostEstimate(
            flops=2 * 2 * BLK * width * 2 * DH * steps, bytes_accessed=width * 2 * DH * steps * 2, transcendentals=0
        ),
        name="project_kv" if for_keys else "project_q",
    )(x0, x1, w, low, up, cosine, sine)
    return made if makes_mid else made[0]


def sort_kernel(source, a, b, c, d, out):
    for slot in range(H):
        pick = source[slot]
        which = pick // 8
        inner = pick % 8
        for k, ref in enumerate((a, b, c, d)):

            @pl.when(which == k)
            def _(ref=ref):
                out[slot // 4, slot % 4] = ref[inner]


def sort_heads(source, parts):
    return pl.pallas_call(
        sort_kernel,
        in_specs=[pl.BlockSpec(memory_space=pltpu.SMEM)] + [pl.BlockSpec(memory_space=pltpu.VMEM)] * 4,
        out_specs=pl.BlockSpec(memory_space=pltpu.VMEM),
        out_shape=jax.ShapeDtypeStruct((KV, 4, BLK, DH), BF),
        compiler_params=pltpu.CompilerParams(vmem_limit_bytes=16 * 2**20),
        cost_estimate=pl.CostEstimate(flops=0, bytes_accessed=2 * H * BLK * DH * 2, transcendentals=0),
        name="sort_heads",
    )(source, *parts)


def unsort_kernel(slots, a, out):
    for head in range(H):
        slot = slots[head]
        out[:, head * DH:(head + 1) * DH] = a[slot // 4, slot % 4]


def unsort_heads(slots, a):
    return pl.pallas_call(
        unsort_kernel,
        in_specs=[pl.BlockSpec(memory_space=pltpu.SMEM), pl.BlockSpec(memory_space=pltpu.VMEM)],
        out_specs=pl.BlockSpec(memory_space=pltpu.VMEM),
        out_shape=jax.ShapeDtypeStruct((BLK, H * DH), BF),
        compiler_params=pltpu.CompilerParams(vmem_limit_bytes=16 * 2**20),
        cost_estimate=pl.CostEstimate(flops=0, bytes_accessed=2 * H * BLK * DH * 2, transcendentals=0),
        name="unsort_heads",
    )(slots, a)


def attend_kernel(blocks, starts, own, q_ref, kv, out, pairs, sems, top, total, acc, floor):
    yh = own[0]

    def copy_of(z):
        return pltpu.make_async_copy(
            kv.at[:, pl.ds((own[1] - z + NZ) % NZ, 1)], pairs.at[:, pl.ds(z, 1)], sems.at[z]
        )

    for z in range(NZ):
        copy_of(z).start()

    def gathered(begin_block, width, kind):
        parts = []
        for k in range(width):
            key_block = jnp.maximum(begin_block + k, 0)
            low = (key_block // (NC * NYH * NX)) % NYL
            stage = ((key_block // NC) % NYH) ^ yh
            source = (((key_block // (NC * NYH)) % NX) * NYL + (low ^ stage)) * NC + key_block % NC
            parts.append(pairs[source, key_block // (NC * NYH * NX * NYL), stage, kind])
        return jnp.concatenate(parts, axis=0)

    def one_tile(tile):
        rows = 4 * BLK
        block = blocks[tile]
        first = block * BLK

        def start_of(place):
            found = jnp.int32(0)
            for d in range(1, DOCS):
                found = jnp.maximum(found, jnp.where(starts[d] <= place, starts[d], 0))
            return found

        span = block + 1 - start_of(first) // BLK
        latest_start = start_of(first + BLK - 1)
        factor = (DH ** -0.5) * 1.4426950408889634

        top[...] = jnp.full(top.shape, NEG_BIG, F32)
        total[...] = jnp.zeros(total.shape, F32)
        acc[...] = jnp.zeros(acc.shape, F32)
        q = q_ref[tile].reshape(rows, DH)

        place = first + lax.broadcasted_iota(jnp.int32, (rows, DH), 0) % BLK
        begin = jnp.zeros((rows, DH), jnp.int32)
        for d in range(1, DOCS):
            begin = jnp.maximum(begin, jnp.where(place >= starts[d], starts[d], 0))
        floor[...] = begin

        def step(begin_block, width, at_end, at_start):
            k_tile = gathered(begin_block, width, 0)
            v_tile = gathered(begin_block, width, 1)
            scores = lax.dot_general(q, k_tile, (((1,), (1,)), ((), ())), preferred_element_type=F32)
            parts = [scores[:, j:j + DH] * factor for j in range(0, width * BLK, DH)]
            lane = lax.broadcasted_iota(jnp.int32, (rows, DH), 1)
            if at_start:
                lowest = floor[...] - lane
                parts = [jnp.where(lowest <= (begin_block + j) * BLK, part, -jnp.inf) for j, part in enumerate(parts)]
            if at_end:
                place = (begin_block + width - 1) * BLK + lane
                inside = place <= first + lax.broadcasted_iota(jnp.int32, (rows, DH), 0) % BLK
                parts[-1] = jnp.where(inside, parts[-1], -jnp.inf)
            old = top[...]
            peak = functools.reduce(jnp.maximum, parts)
            new = jnp.maximum(old, jnp.max(peak, axis=1, keepdims=True))
            shrink = jnp.exp2(old - new)
            powers = [jnp.exp2(part - new) for part in parts]
            top[...] = new
            total[...] = total[...] * shrink + functools.reduce(jnp.add, powers)
            weights = jnp.concatenate([p.astype(BF) for p in powers], axis=1)
            acc[...] = acc[...] * shrink + jnp.dot(weights, v_tile, preferred_element_type=F32)

        whole_steps = (span + TAIL - 1) // WIDE

        def body(index, carry):
            begin_block = block + 1 - WIDE * (index + 1)
            early = begin_block * BLK < latest_start

            @pl.when(early)
            def _():
                step(begin_block, WIDE, True, True)

            @pl.when(jnp.logical_not(early) & (index == 0))
            def _():
                step(begin_block, WIDE, True, False)

            @pl.when(jnp.logical_not(early) & (index > 0))
            def _():
                step(begin_block, WIDE, False, False)

            return carry

        lax.fori_loop(0, whole_steps, body, 0)

        left = span - WIDE * whole_steps
        for width in range(TAIL, WIDE, TAIL):

            @pl.when((left > width - TAIL) & (left <= width))
            def _(width=width):
                step(block + 1 - WIDE * whole_steps - width, width, True, True)

        out[tile] = (acc[...] / jnp.sum(total[...], axis=1, keepdims=True)).astype(BF).reshape(4, BLK, DH)

    def pair(z, carry):
        copy_of(z).wait()
        one_tile(2 * z)
        one_tile(2 * z + 1)
        return carry

    lax.fori_loop(0, NZ, pair, 0)


def attend(blocks, starts, own, q, kv):
    rows = 4 * BLK
    return pl.pallas_call(
        attend_kernel,
        in_specs=[pl.BlockSpec(memory_space=pltpu.SMEM)] * 3
        + [
            pl.BlockSpec(memory_space=pltpu.VMEM),
            pl.BlockSpec(memory_space=pl.ANY),
        ],
        out_specs=pl.BlockSpec(memory_space=pltpu.VMEM),
        out_shape=jax.ShapeDtypeStruct((8, 4, BLK, DH), BF),
        scratch_shapes=[
            pltpu.VMEM((NX * NYL * NC, NZ, 2, 2, BLK, DH), BF),
            pltpu.SemaphoreType.DMA((NZ,)),
            pltpu.VMEM((rows, DH), F32),
            pltpu.VMEM((rows, DH), F32),
            pltpu.VMEM((rows, DH), F32),
            pltpu.VMEM((rows, DH), jnp.int32),
        ],
        compiler_params=pltpu.CompilerParams(vmem_limit_bytes=60 * 2**20),
        cost_estimate=pl.CostEstimate(flops=10**10, bytes_accessed=10 * 2**20, transcendentals=10**7),
        name="attend",
    )(blocks, starts, own, q, kv)


def per_device(tokens, w, down, up, document_index, query_to_key_head):
    z, yl, x, yh, c = (lax.axis_index(a) for a in ALL)
    block = flat(z, yl, x, yh, c)
    far_block = flat(z, 1 - yl, x, 1 - yh, c)
    other = 1 - 2 * c

    far = lax.ppermute(tokens, ALL, CROSS)
    near_pair = lax.ppermute(tokens, "c", SWAP)

    near_cos, near_sin = rope_tables(jnp.stack([block, block + other]))
    far_cos, far_sin = rope_tables(jnp.stack([far_block, far_block + other]))

    def split_kv(near, far, beside):
        mine, theirs = jnp.stack([near[0], far[0]], 1), lax.ppermute(jnp.stack([near[1], far[1]], 1), "c", SWAP)
        heads = jnp.where(c == 0, jnp.concatenate([mine, theirs], 0), jnp.concatenate([theirs, mine], 0))
        rows = []
        for k in range(NZ):
            head = lax.dynamic_index_in_dim(heads, (z + k) % NZ, 0, keepdims=False)
            rows.append(lax.ppermute(head, "z", [(i, (i + k) % NZ) for i in range(NZ)]) if k else head)
        rows, beside = lax.optimization_barrier((rows, beside))
        return jnp.stack(rows)[None], beside

    q_near, kv_near = project_both(tokens, near_pair, w, down, up, near_cos, near_sin)
    far, q_near, kv_near = lax.optimization_barrier((far, q_near, kv_near))
    far_pair = lax.ppermute(far, "c", SWAP)
    kv_far, mid_far = project(True, far, far_pair, w, down, up, far_cos, far_sin)
    q_far = project(False, far, far_pair, w, mid_far, up, far_cos, far_sin)
    rows, q_far = split_kv(kv_near, kv_far, q_far)
    kv = lax.all_gather(rows, ("x", "yl", "c"), axis=0, tiled=True)
    home_c = lax.ppermute(q_far[0], ALL, CROSS)
    home_d = lax.ppermute(q_far[1], ALL, CROSS_OTHER)

    parts = (
        q_near[0],
        lax.ppermute(q_near[1], "c", SWAP),
        home_c,
        home_d,
    )
    member = (query_to_key_head % 4) * 2 + query_to_key_head // 4
    heads = jnp.arange(H, dtype=jnp.int32)
    same = (member[None, :] == member[:, None]) & (heads[None, :] < heads[:, None])
    slots = member * 4 + jnp.sum(same.astype(jnp.int32), axis=1)
    source_of_head = ((heads // 8) ^ (yh * 2 + c)) * 8 + heads % 8
    source = jnp.sum(jnp.where(slots[None, :] == heads[:, None], source_of_head[None, :], 0), axis=1)
    sorted_q = sort_heads(source, parts)
    q = lax.all_to_all(sorted_q, ALL, split_axis=0, concat_axis=0, tiled=True, axis_index_groups=GROUPS)

    member_z = jnp.arange(8, dtype=jnp.int32) // 2
    member_yh = jnp.arange(8, dtype=jnp.int32) % 2
    blocks = flat(member_z, (yl ^ yh) ^ member_yh, (x - z + member_z) % NX, member_yh, c).astype(jnp.int32)
    starts = jnp.sum(
        (document_index[None, :] < jnp.arange(DOCS, dtype=jnp.int32)[:, None]).astype(jnp.int32), axis=1
    )
    context = attend(blocks, starts, jnp.stack([yh, z]).astype(jnp.int32), q, kv)
    home = lax.all_to_all(context, ALL, split_axis=0, concat_axis=0, tiled=True, axis_index_groups=GROUPS)
    return unsort_heads(slots, home)


def solution(mesh):
    fine = Mesh(mesh.devices.reshape(NZ, NYL, NX, NYH, NC), ALL)
    return jax.shard_map(
        per_device,
        mesh=fine,
        in_specs=(P(ALL, None), P(None, ("yh", "c")), P(), P(None, ("yh", "c")), P(), P()),
        out_specs=P(ALL, None),
        check_vma=False,
    )
```
